512 devices in a mesh: row: 32 (over z, core), col: 16 (over y, x).
Axes of the slice: x: 4, y: 4, z: 16, core: 2. Of those that a mesh axis runs over, the one named last changes fastest.
Arguments:
- a_blocks: bfloat16 [32, 16, 96, 128, 128], P('row', 'col'), may hold values from -0.5 to 0.5
- a_rows: int32 [32, 16, 96], P('row', 'col'), may hold values from 0 to 31, as said below
- a_cols: int32 [32, 16, 96], P('row', 'col'), may hold values from 0 to 63, as said below
- p_blocks: bfloat16 [1024, 128, 256], P(('row', 'col')), may hold values from -0.5 to 0.5
- coarse_slot: int32 [32, 16, 96, 4, 4], P('row', 'col'), may hold values from 0 to 127
Outputs:
- coarse_blocks: bfloat16 [32, 128, 4096], P('row', 'col')
The draws below stay inside these ranges and needn't reach their ends.
Inputs may be any that keep to these rules, and one draw needn't show every extreme that they name: On each owner the pairs (a_rows, a_cols) of its 96 blocks are distinct. On each owner the pairs (a_rows, a_cols) of its 96 blocks are distinct.
All inputs are finite; a program needn't handle non-finite values.
Results may differ from the reference program's by a relative error of at most 0.0049.
Values may be sent and summed in bfloat16 or wider, within the bound.
A program may use at most 128 MiB of HBM per device.

```python
import jax
import jax.numpy as jnp
from jax import lax

NODE = 128
AGG = 64
KP = 4
FQ = 2
KA = 96
FR = 32
FC = 64
NF = 1024
KS = 128
N_ROW = 32
N_COL = 16


def pattern(key):
    folded = jax.random.fold_in(key, 7)
    device_keys = jax.random.split(folded, N_ROW * N_COL)

    def draw_one(subkey):
        shuffled = jax.random.permutation(subkey, FR * FC)
        return shuffled[:KA].astype(jnp.int32)
    return jax.vmap(draw_one)(device_keys).reshape(N_ROW, N_COL, KA)


def draw_a_rows(key, part):
    return (pattern(key) // FC).astype(jnp.int32)


def draw_a_cols(key, part):
    return (pattern(key) % FC).astype(jnp.int32)


def touch_ends(entries, rng, low, high):
    index_at = [jax.random.randint(jax.random.fold_in(rng, axis), (), 0, length) for axis, length in enumerate(entries.shape)]
    longest = entries.shape.index(max(entries.shape))
    beside = index_at[:longest] + [(index_at[longest] + 1) % entries.shape[longest]] + index_at[longest + 1:]
    return entries.at[tuple(index_at)].set(low).at[tuple(beside)].set(high)


def block_scale(rng, shape, cuts, smallest, high):
    def one(axis_at, shards_of):
        heights = jax.random.uniform(jax.random.fold_in(jax.random.fold_in(rng, 6), axis_at), (shards_of,), jnp.float32, smallest / len(cuts), high / len(cuts))
        return jnp.repeat(jnp.exp(heights), shape[axis_at] // shards_of).reshape((-1,) + (1,) * (len(shape) - axis_at - 1))

    loudness = one(*cuts[0])
    for cut in cuts[1:]:
        loudness = loudness * one(*cut)
    return loudness


def centred(stream_key, extent, spread, limit, cuts=(), kind=jnp.bfloat16):
    result = jax.random.normal(stream_key, extent, jnp.float32) * spread
    if len(cuts) > 0:
        result = block_scale(stream_key, extent, cuts, -0.22, 0.18) * result
    return jnp.clip(result, min=-limit, max=limit).astype(kind)


def setup_inputs(seed: int = 0) -> dict:
    keys = jax.random.split(jax.random.key(seed), 6)
    a_blocks = centred(keys[0], (N_ROW, N_COL, KA, NODE, NODE), NODE ** -0.5, 0.5, ((0, 32), (1, 16)))
    a_rows = draw_a_rows(jax.random.fold_in(keys[5], 71), 0)
    a_cols = draw_a_cols(jax.random.fold_in(keys[5], 71), 0)
    p_blocks = centred(keys[3], (NF, NODE, KP * AGG), NODE ** -0.5, 0.5, ((0, 512),))
    coarse_slot = touch_ends(jax.random.randint(keys[4], (N_ROW, N_COL, KA, KP, KP), 0, KS), jax.random.fold_in(keys[4], 1), 0, KS - 1).astype(jnp.int32)
    return dict(a_blocks=a_blocks, a_rows=a_rows, a_cols=a_cols, p_blocks=p_blocks, coarse_slot=coarse_slot)


def owner_terms(blocks, row_ids, col_ids, slot_ids, row_panel, column_panel):
    count = blocks.shape[0]
    group_size = 16 if count % 16 == 0 else 8 if count % 8 == 0 else 1
    groups = count // group_size
    node_width = blocks.shape[1]
    panel_width = row_panel.shape[2]
    agg_blocks = slot_ids.shape[1]
    agg_width = panel_width // agg_blocks

    def accumulate(running, batch_item):
        blk, rws, cls, sls = batch_item
        right_rows = jnp.take(column_panel, cls, axis=0)
        product = jnp.einsum("kab,kbw->kaw", blk.astype(jnp.float32), right_rows.astype(jnp.float32)).astype(jnp.bfloat16)
        left_rows = jnp.take(row_panel, rws, axis=0)
        left_split = left_rows.reshape(group_size, node_width, agg_blocks, agg_width).astype(jnp.float32)
        right_split = product.reshape(group_size, node_width, agg_blocks, agg_width).astype(jnp.float32)
        contribs = jnp.einsum("knta,knsb->ktsab", left_split, right_split)
        contribs = contribs.reshape(group_size * agg_blocks * agg_blocks, agg_width * agg_width)
        running = running.at[sls.reshape(-1)].add(contribs)
        return running, None

    items = (blocks.reshape(groups, group_size, node_width, node_width),
             row_ids.reshape(groups, group_size),
             col_ids.reshape(groups, group_size),
             slot_ids.reshape(groups, group_size, agg_blocks, agg_blocks))
    start = jnp.zeros((KS, agg_width * agg_width), jnp.float32)
    running, _ = lax.scan(accumulate, start, items)
    return running


def reference(a_blocks, a_rows, a_cols, p_blocks, coarse_slot):
    row_span = N_COL * FQ
    col_span = N_ROW * FQ

    def per_row(row_index):
        row_panel = lax.dynamic_slice_in_dim(p_blocks, row_index * row_span, row_span, 0)

        def per_col(running, col_index):
            column_panel = lax.dynamic_slice_in_dim(p_blocks, col_index * col_span, col_span, 0)
            blocks = a_blocks[row_index, col_index]
            row_ids = a_rows[row_index, col_index].astype(jnp.int32)
            col_ids = a_cols[row_index, col_index].astype(jnp.int32)
            slot_ids = coarse_slot[row_index, col_index].astype(jnp.int32)
            return running + owner_terms(blocks, row_ids, col_ids, slot_ids, row_panel, column_panel), None

        start = jnp.zeros((KS, AGG * AGG), jnp.float32)
        running, _ = lax.scan(per_col, start, jnp.arange(N_COL, dtype=jnp.int32))
        return running.astype(jnp.bfloat16)

    return lax.map(per_row, jnp.arange(N_ROW, dtype=jnp.int32))
```

```python
import functools

import jax
import jax.numpy as jnp
from jax import lax
from jax.experimental import pallas as pl
from jax.experimental.pallas import tpu as pltpu
from jax.sharding import PartitionSpec as P

MESH = pl.DeviceIdType.MESH
BF16, F32 = jnp.bfloat16, jnp.float32

HOP = 2
HALVES = 2


def gray(v):
    return v + v // 2 - 2 * ((v // 2) * (v % 2))


def panels_kernel(dims, p_ref, row_ref, col_ref, own_sem, send_sem, row_sem, z_send, z_recv, s_send, s_recv, c_sem):
    nz, ny, nx = dims
    ncol = ny * nx
    r, c = lax.axis_index("row"), lax.axis_index("col")
    z, core = r // 2, r % 2
    y, x = c // nx, c % nx
    up, down = 2 * ((z + 1) % nz) + core, 2 * ((z + nz - 1) % nz) + core
    sibling = 2 * z + 1 - core
    half = p_ref.shape[1] // HALVES
    base = core * 2 * ncol
    steps_x = [gray(v) for v in range(1, nx)]
    steps_y = [gray(v) for v in range(1, ny)]

    def along_x(d):
        return y * nx + (x + d) % nx

    def along_y(d):
        return ((y + d) % ny) * nx + x

    barrier = pltpu.get_barrier_semaphore()
    peers = [(r, along_x(d)) for d in steps_x] + [(r, along_y(d)) for d in steps_y]
    peers += [(up, c), (down, c), (sibling, c)]
    for peer in peers:
        pl.semaphore_signal(barrier, inc=1, device_id=peer, device_id_type=MESH)
    pl.semaphore_wait(barrier, len(peers))

    def row_copy(src, row, slot, target):
        return pltpu.make_async_remote_copy(
            src_ref=src,
            dst_ref=row_ref.at[row],
            send_sem=send_sem.at[slot],
            recv_sem=row_sem.at[row],
            device_id=(r, target),
            device_id_type=MESH,
        )

    sends = []

    def give(src, row, target):
        copy = row_copy(src, row, len(sends), target)
        copy.start()
        sends.append(copy)

    def arrived(row):
        row_copy(row_ref.at[row], row, 0, c).wait_recv()

    hops_up, hops_down = (z - c + nz) % nz, (c - z + nz) % nz
    root = hops_up == 0
    count = ncol * HALVES

    def row_up(q):
        u, v = gray(q // nx), gray(q % nx)
        return 2 * (((y + u) % ny) * nx + (x + v) % nx)

    def row_down(q):
        u, v = gray(q // ny), gray(q % ny)
        return 2 * (((y + v) % ny) * nx + (x + u) % nx) + 1

    def part(ref, row, h):
        return ref.at[row, pl.ds(pl.multiple_of(h * half, half), half)]

    def place(way, n):
        q, h = n // HALVES, n % HALVES
        return (row_up(q) if way == 0 else row_down(q)), h

    def z_copy(way, n, from_root):
        row, h = place(way, n)
        return pltpu.make_async_remote_copy(
            src_ref=part(row_ref, row, h) if from_root else part(col_ref, base + row, h),
            dst_ref=part(col_ref, base + row, h),
            send_sem=z_send.at[way, n],
            recv_sem=z_recv.at[way, n],
            device_id=(up if way == 0 else down, c),
            device_id_type=MESH,
        )

    def s_copy(way, n, from_root):
        row, h = place(way, n)
        return pltpu.make_async_remote_copy(
            src_ref=part(row_ref, row, h) if from_root else part(col_ref, base + row, h),
            dst_ref=part(col_ref, base + row, h),
            send_sem=s_send.at[way, n],
            recv_sem=s_recv.at[way, n],
            device_id=(sibling, c),
            device_id_type=MESH,
        )

    def c_copy(way, n):
        row, h = place(way, n)
        return pltpu.make_async_copy(part(row_ref, row, h), part(col_ref, base + row, h), c_sem.at[way, n])

    def from_root(way, n):
        z_copy(way, n, True).start()
        s_copy(way, n, True).start()
        c_copy(way, n).start()

    def relay(way, n):
        hops = hops_up if way == 0 else hops_down

        @pl.when(root & (n >= HALVES))
        def _():
            @pl.when((n % HALVES == 0) & (n >= HALVES * (nx if way == 0 else ny)))
            def _():
                arrived(place(way, n)[0])

            from_root(way, n)

        @pl.when(jnp.logical_not(root))
        def _():
            z_copy(way, n, False).wait_recv()

            @pl.when(hops < nz - 1)
            def _():
                z_copy(way, n, False).start()

            s_copy(way, n, False).start()

    mine = pltpu.make_async_copy(p_ref, row_ref.at[pl.ds(2 * c, 2)], own_sem)
    mine.start()
    for i in range(max(nx, ny) - 1):
        if i < nx - 1:
            give(p_ref.at[0], 2 * c, along_x(steps_x[i]))
        if i < ny - 1:
            give(p_ref.at[1], 2 * c + 1, along_y(steps_y[i]))
    mine.wait()

    @pl.when(root)
    def _():
        for n in range(HALVES):
            from_root(0, n)
            from_root(1, n)

    for d in steps_y:
        give(p_ref.at[0], 2 * c, along_y(d))
    for d in steps_x:
        give(p_ref.at[1], 2 * c + 1, along_x(d))
    for i in range(max(nx, ny) - 1):
        if i < nx - 1:
            row = 2 * along_x(steps_x[i])
            arrived(row)
            for d in steps_y:
                give(row_ref.at[row], row, along_y(d))
        if i < ny - 1:
            row = 2 * along_y(steps_y[i]) + 1
            arrived(row)
            for d in steps_x:
                give(row_ref.at[row], row, along_x(d))

    @pl.loop(0, count + HOP * (nz - 1))
    def _(step):
        n_up, n_down = step - HOP * hops_up, step - HOP * hops_down

        @pl.when((n_up >= 0) & (n_up < count))
        def _():
            relay(0, n_up)

        @pl.when((n_down >= 0) & (n_down < count))
        def _():
            relay(1, n_down)

    @pl.when(jnp.logical_not(root))
    def _():
        @pl.loop(nx, ncol)
        def _(q):
            arrived(row_up(q))

        @pl.loop(ny, ncol)
        def _(q):
            arrived(row_down(q))

    for copy in sends:
        copy.wait_send()

    @pl.loop(0, count)
    def _(n):
        for way, hops in ((0, hops_up), (1, hops_down)):
            @pl.when(hops < nz - 1)
            def _():
                z_copy(way, n, False).wait_send()

            s_copy(way, n, False).wait_send()
            s_copy(way, n, False).wait_recv()

            @pl.when(root)
            def _():
                c_copy(way, n).wait()


def panels(p_blocks, dims):
    nz, ny, nx = dims
    ncol = ny * nx
    _, node, width = p_blocks.shape
    count = ncol * HALVES
    vmem = pl.BlockSpec(memory_space=pltpu.VMEM)
    dma = pltpu.SemaphoreType.DMA
    return pl.pallas_call(
        functools.partial(panels_kernel, dims),
        out_shape=(
            jax.ShapeDtypeStruct((2 * ncol, node, width), BF16),
            jax.ShapeDtypeStruct((4 * ncol, node, width), BF16),
        ),
        in_specs=[vmem],
        out_specs=(vmem, vmem),
        scratch_shapes=[
            dma,
            dma((2 * (ncol - 1),)),
            dma((2 * ncol,)),
            dma((2, count)),
            dma((2, count)),
            dma((2, count)),
            dma((2, count)),
            dma((2, count)),
        ],
        compiler_params=pltpu.CompilerParams(collective_id=0, has_side_effects=True, vmem_limit_bytes=24 << 20),
        name="panels",
    )(p_blocks)


GROUP = 4


def terms_kernel(rows_ref, cols_ref, slots_ref, a_ref, row_ref, col_ref, out_ref, left, *totals):
    count = a_ref.shape[0]
    panel_rows, node, width = row_ref.shape
    kp = len(totals)
    agg = width // kp
    half = agg // 2

    for total in totals:
        total[...] = jnp.zeros_like(total)

    to = lax.broadcasted_iota(jnp.int32, (width, width), 0)
    at = lax.broadcasted_iota(jnp.int32, (width, width), 1)
    inner = to % agg
    source = to - inner + 2 * (inner % half) + inner // half
    pick = jnp.where(at == source, 1.0, 0.0).astype(BF16)

    @pl.loop(0, panel_rows, unroll=2)
    def _(i):
        left[i] = lax.dot_general(
            pick, row_ref[i], (((1,), (1,)), ((), ())), preferred_element_type=F32
        ).astype(BF16)

    low = lax.broadcasted_iota(jnp.int32, (half, 2 * agg), 1) < agg

    def block(k):
        product = jnp.dot(a_ref[k], col_ref[cols_ref[k]], preferred_element_type=F32).astype(BF16)
        term = jnp.dot(left[rows_ref[k]], product, preferred_element_type=F32)
        for pair in range(kp // 2):
            lanes = slice(pair * 2 * agg, (pair + 1) * 2 * agg)
            for t in range(kp):
                even = term[t * agg : t * agg + half, lanes]
                odd = term[t * agg + half : (t + 1) * agg, lanes]
                total = totals[t]
                slot = slots_ref[(k * kp + t) * kp + 2 * pair]
                total[slot] += jnp.where(low, even, pltpu.roll(odd, agg, 1))
                slot = slots_ref[(k * kp + t) * kp + 2 * pair + 1]
                total[slot] += jnp.where(low, pltpu.roll(even, agg, 1), odd)

    @pl.loop(0, count // GROUP)
    def _(g):
        for i in range(GROUP):
            block(g * GROUP + i)

    @pl.loop(0, out_ref.shape[0] // 8)
    def _(g):
        some = pl.ds(pl.multiple_of(g * 8, 8), 8)
        out_ref[some] = functools.reduce(lambda p, q: p + q, [total[some] for total in totals]).astype(BF16)


def local_terms(a_blocks, a_rows, a_cols, slots, row_panel, col_panel, slot_count):
    panel_rows, node, width = row_panel.shape
    kp = slots.shape[1]
    agg = width // kp
    vmem, smem = pl.BlockSpec(memory_space=pltpu.VMEM), pl.BlockSpec(memory_space=pltpu.SMEM)
    return pl.pallas_call(
        terms_kernel,
        out_shape=jax.ShapeDtypeStruct((slot_count, agg // 2, 2 * agg), BF16),
        in_specs=[smem, smem, smem, vmem, vmem, vmem],
        out_specs=vmem,
        scratch_shapes=[pltpu.VMEM((panel_rows, width, node), BF16)]
        + [pltpu.VMEM((slot_count, agg // 2, 2 * agg), F32)] * kp,
        compiler_params=pltpu.CompilerParams(vmem_limit_bytes=48 << 20),
        name="terms",
    )(a_rows, a_cols, slots.reshape(-1), a_blocks, row_panel, col_panel)


def sums_kernel(ncol, part_ref, out_ref, landed, own_sem, send_sem, recv_sem):
    r, c = lax.axis_index("row"), lax.axis_index("col")
    share = out_ref.shape[0]
    barrier = pltpu.get_barrier_semaphore()
    for d in range(1, ncol):
        pl.semaphore_signal(barrier, inc=1, device_id=(r, (c + d) % ncol), device_id_type=MESH)
    pl.semaphore_wait(barrier, ncol - 1)

    def copy(d):
        target = (c + d) % ncol
        return pltpu.make_async_remote_copy(
            src_ref=part_ref.at[pl.ds(target * share, share)],
            dst_ref=landed.at[d],
            send_sem=send_sem.at[d],
            recv_sem=recv_sem.at[d],
            device_id=(r, target),
            device_id_type=MESH,
        )

    for d in range(1, ncol):
        copy(d).start()
    mine = pltpu.make_async_copy(part_ref.at[pl.ds(c * share, share)], landed.at[0], own_sem)
    mine.start()
    mine.wait()
    for d in range(1, ncol):
        copy(d).wait_recv()
    for d in range(1, ncol):
        copy(d).wait_send()
    rows, lanes = landed.shape[2:]
    total = landed[0].astype(F32)
    for d in range(1, ncol):
        total = total + landed[d].astype(F32)
    for i in range(rows):
        out_ref[:, i * lanes : (i + 1) * lanes] = total[:, i, :].astype(BF16)


def sum_at_owner(partial, ncol):
    slots, rows, lanes = partial.shape
    share = slots // ncol
    vmem = pl.BlockSpec(memory_space=pltpu.VMEM)
    dma = pltpu.SemaphoreType.DMA
    return pl.pallas_call(
        functools.partial(sums_kernel, ncol),
        out_shape=jax.ShapeDtypeStruct((share, rows * lanes), BF16),
        in_specs=[vmem],
        out_specs=vmem,
        scratch_shapes=[
            pltpu.VMEM((ncol, share, rows, lanes), BF16),
            dma,
            dma((ncol,)),
            dma((ncol,)),
        ],
        compiler_params=pltpu.CompilerParams(collective_id=1, has_side_effects=True, vmem_limit_bytes=16 << 20),
        name="sums",
    )(partial)


def on_device(dims, slot_count, a_blocks, a_rows, a_cols, p_blocks, coarse_slot):
    ncol = dims[1] * dims[2]
    row_panel, col_panel = panels(p_blocks, dims)
    partial = local_terms(
        a_blocks[0, 0], a_rows[0, 0], a_cols[0, 0], coarse_slot[0, 0], row_panel, col_panel, slot_count
    )
    return sum_at_owner(partial, ncol)[None]


def solution(mesh, dims=(16, 4, 4), slot_count=128):
    placed = (
        P("row", "col", None, None, None),
        P("row", "col", None),
        P("row", "col", None),
        P(("row", "col"), None, None),
        P("row", "col", None, None, None),
    )
    return jax.shard_map(
        functools.partial(on_device, dims, slot_count),
        mesh=mesh,
        in_specs=placed,
        out_specs=P("row", "col", None),
        check_vma=False,
    )
```

```python
import functools

import jax
import jax.numpy as jnp
from jax import lax
from jax.experimental import pallas as pl
from jax.experimental.pallas import tpu as pltpu
from jax.sharding import PartitionSpec as P

MESH = pl.DeviceIdType.MESH
BF16, F32 = jnp.bfloat16, jnp.float32

HOP = 4
KP = 4
GROUP = 16
PARTS = 2


def gray(v):
    return v + v // 2 - 2 * ((v // 2) * (v % 2))


def panels_kernel(dims, p_ref, row_ref, col_ref, passing, own_sem, g_send, g_recv, r_send, r_recv, z_send, z_recv, a_send, a_recv, s_send, s_recv):
    nz, ny, nx = dims
    ncol = ny * nx
    r, c = lax.axis_index("row"), lax.axis_index("col")
    z, core = r // 2, r % 2
    y, x = c // nx, c % nx
    up, down = 2 * ((z + 1) % nz) + core, 2 * ((z + nz - 1) % nz) + core
    sibling = 2 * z + 1 - core
    base = core * 2 * ncol
    far = nz // 2
    steps_x = [gray(v) for v in range(1, nx)]
    steps_y = [gray(v) for v in range(1, ny)]

    def along_x(d):
        return y * nx + (x + d) % nx

    def along_y(d):
        return ((y + d) % ny) * nx + x

    barrier = pltpu.get_barrier_semaphore()
    peers = [(r, along_x(d)) for d in steps_x] + [(r, along_y(d)) for d in steps_y]
    peers += [(up, c), (down, c), (sibling, c)]
    for peer in peers:
        pl.semaphore_signal(barrier, inc=1, device_id=peer, device_id_type=MESH)
    pl.semaphore_wait(barrier, len(peers))

    def remote(src, dst, send, recv, device):
        return pltpu.make_async_remote_copy(
            src_ref=src, dst_ref=dst, send_sem=send, recv_sem=recv, device_id=device, device_id_type=MESH
        )

    root = x == z % nx
    plane = z // nx

    def gather_copy(x0):
        return remote(p_ref, passing.at[plane, x0], g_send, g_recv.at[x0], (r, y * nx + z % nx))

    part = p_ref.shape[1] // PARTS

    def z_copy(way, y1, x0, j):
        here = passing.at[y1, x0, j // PARTS, pl.ds(pl.multiple_of(j % PARTS * part, part), part)]
        return remote(here, here, z_send.at[way, y1, x0, j], z_recv.at[way, y1, x0, j], (up if way == 0 else down, c))

    def name(way, pos):
        o = pos if way == 0 else (nx - pos) % nx
        return (x + o) % nx, (o < nx // 2 if way == 0 else o >= nx // 2)

    def a_copy(y1, x0):
        rows = col_ref.at[pl.ds(base + 2 * (y * nx + x0), 2)]
        return remote(passing.at[y1, x0], rows, a_send.at[y1, x0], a_recv.at[y * nx + x0], (r, y1 * nx + x))

    def deliver(y1, x0):
        @pl.when(y1 != y)
        def _():
            a_copy(y1, x0).start()

        @pl.when(y1 == y)
        def _():
            rows = col_ref.at[pl.ds(base + 2 * (y * nx + x0), 2)]
            pltpu.make_async_copy(passing.at[y1, x0], rows, a_recv.at[y * nx + x0]).start()

    sends = []

    def give(src, piece, target):
        rows = row_ref.at[pl.ds(2 * piece, 2)]
        copy = remote(src, rows, r_send.at[len(sends)], r_recv.at[piece], (r, target))
        copy.start()
        sends.append(copy)

    def arrived(piece):
        rows = row_ref.at[pl.ds(2 * piece, 2)]
        remote(rows, rows, r_send.at[0], r_recv.at[piece], (r, c)).wait_recv()

    @pl.when(jnp.logical_not(root))
    def _():
        gather_copy(x).start()

    @pl.when(root)
    def _():
        copy = pltpu.make_async_copy(p_ref, passing.at[plane, x], own_sem.at[1])
        copy.start()
        copy.wait()
        for j in range(2 * PARTS):
            z_copy(0, plane, x, j).start()
            z_copy(1, plane, x, j).start()
        deliver(plane, x)

    mine = pltpu.make_async_copy(p_ref, row_ref.at[pl.ds(2 * c, 2)], own_sem.at[0])
    mine.start()
    for d in steps_y:
        give(p_ref, c, along_y(d))
    for d in steps_x:
        give(p_ref, c, along_x(d))

    @pl.when(root)
    def _():
        for pos in range(1, nx):
            a, b = name(0, pos)[0], name(1, pos)[0]
            if 2 * pos <= nx:
                gather_copy(a).wait_recv()
                if 2 * pos < nx:
                    gather_copy(b).wait_recv()
            for j in range(2 * PARTS):
                z_copy(0, plane, a, j).start()
                z_copy(1, plane, b, j).start()
            deliver(plane, a)

    for d in steps_y:
        piece = along_y(d)
        arrived(piece)
        for e in steps_x:
            give(row_ref.at[pl.ds(2 * piece, 2)], piece, along_x(e))

    near_up = (z - x + nz - 1) % nx + 1
    near_down = (x - z + nz - 1) % nx + 1
    feeds, parts = far // nx, 2 * PARTS
    chunks = nx * parts

    def chunk(way, feed, n):
        dist = (near_up if way == 0 else near_down) + nx * feed
        z0 = (z - dist + nz) % nz if way == 0 else (z + dist) % nz
        x0, opposite = name(way, n // parts)
        comes = (dist < far) | ((dist == far) & opposite)
        goes = (dist < far - 1) | ((dist == far - 1) & opposite)
        return z0 // nx, x0, n % parts, comes, goes

    def relay(way, feed, n):
        y1, x0, j, comes, goes = chunk(way, feed, n)

        @pl.when(comes)
        def _():
            z_copy(way, y1, x0, j).wait_recv()

            @pl.when(goes)
            def _():
                z_copy(way, y1, x0, j).start()

            @pl.when(j == parts - 1)
            def _():
                deliver(y1, x0)

    @pl.loop(0, chunks + HOP * (far - 1))
    def _(step):
        for feed in range(feeds):
            for way, near in ((0, near_up), (1, near_down)):
                n = step - HOP * (near + nx * feed - 1)

                @pl.when((n >= 0) & (n < chunks))
                def _():
                    relay(way, feed, n)

    def s_copy(c0):
        rows = col_ref.at[pl.ds(base + 2 * c0, 2)]
        return remote(rows, rows, s_send.at[c0], s_recv.at[c0], (sibling, c))

    @pl.loop(0, ncol)
    def _(i):
        c0 = (c + i) % ncol
        rows = col_ref.at[pl.ds(base + 2 * c0, 2)]
        remote(passing.at[0, 0], rows, a_send.at[0, 0], a_recv.at[c0], (r, c)).wait_recv()
        s_copy(c0).start()

    for u in range(ny):
        for v in range(1, nx):
            arrived(((y + u) % ny) * nx + (x + v) % nx)
    mine.wait()
    for copy in sends:
        copy.wait_send()

    @pl.when(jnp.logical_not(root))
    def _():
        gather_copy(x).wait_send()

    @pl.loop(0, nx)
    def _(x0):
        @pl.when(root)
        def _():
            for j in range(2 * PARTS):
                z_copy(0, plane, x0, j).wait_send()
                z_copy(1, plane, x0, j).wait_send()

        for y1 in range(ny):
            @pl.when(y1 != y)
            def _():
                a_copy(y1, x0).wait_send()

    @pl.loop(0, chunks)
    def _(n):
        for feed in range(feeds):
            for way in (0, 1):
                y1, x0, j, comes, goes = chunk(way, feed, n)

                @pl.when(comes & goes)
                def _():
                    z_copy(way, y1, x0, j).wait_send()

    @pl.loop(0, ncol)
    def _(c0):
        s_copy(c0).wait_send()
        s_copy(c0).wait_recv()


def panels(p_blocks, dims):
    nz, ny, nx = dims
    ncol = ny * nx
    _, node, width = p_blocks.shape
    vmem = pl.BlockSpec(memory_space=pltpu.VMEM)
    dma = pltpu.SemaphoreType.DMA
    return pl.pallas_call(
        functools.partial(panels_kernel, dims),
        out_shape=(
            jax.ShapeDtypeStruct((2 * ncol, node, width), BF16),
            jax.ShapeDtypeStruct((4 * ncol, node, width), BF16),
        ),
        in_specs=[vmem],
        out_specs=(vmem, vmem),
        scratch_shapes=[
            pltpu.VMEM((ny, nx, 2, node, width), BF16),
            dma((2,)),
            dma,
            dma((nx,)),
            dma((ncol - 1,)),
            dma((ncol,)),
            dma((2, ny, nx, 2 * PARTS)),
            dma((2, ny, nx, 2 * PARTS)),
            dma((ny, nx)),
            dma((ncol,)),
            dma((ncol,)),
            dma((ncol,)),
        ],
        compiler_params=pltpu.CompilerParams(collective_id=0, has_side_effects=True, vmem_limit_bytes=16 << 20),
        name="panels",
    )(p_blocks)


def terms_kernel(rows_ref, cols_ref, slots_ref, a_ref, row_ref, col_ref, out_ref, turned, left_ref, *totals):
    count, width, node = left_ref.shape
    panel_rows = row_ref.shape[0]
    agg = width // KP
    half = agg // 2

    @pl.loop(0, out_ref.shape[0] // 8)
    def _(g):
        some = pl.ds(pl.multiple_of(g * 8, 8), 8)
        for total in totals:
            total[some] = jnp.zeros((8, *total.shape[1:]), F32)

    to = lax.broadcasted_iota(jnp.int32, (width, width), 0)
    at = lax.broadcasted_iota(jnp.int32, (width, width), 1)
    inner = to % agg
    source = to - inner + 2 * (inner % half) + inner // half
    pick = jnp.where(at == source, 1.0, 0.0).astype(BF16)

    @pl.loop(0, panel_rows // 8)
    def _(g):
        for i in range(8):
            turned[g * 8 + i] = lax.dot_general(
                pick, row_ref[g * 8 + i], (((1,), (1,)), ((), ())), preferred_element_type=F32
            ).astype(BF16)

    @pl.loop(0, count // GROUP)
    def _(g):
        for i in range(GROUP):
            k = g * GROUP + i
            left_ref[k] = jnp.dot(turned[rows_ref[k]], a_ref[k], preferred_element_type=F32).astype(BF16)

    low = lax.broadcasted_iota(jnp.int32, (half, 2 * agg), 1) < agg

    def block(k):
        term = jnp.dot(left_ref[k], col_ref[cols_ref[k]], preferred_element_type=F32)
        for pair in range(KP // 2):
            lanes = slice(pair * 2 * agg, (pair + 1) * 2 * agg)
            for t in range(KP):
                even = term[t * agg : t * agg + half, lanes]
                odd = term[t * agg + half : (t + 1) * agg, lanes]
                total = totals[t % len(totals)]
                total[slots_ref[t, 2 * pair, k]] += jnp.where(low, even, pltpu.roll(odd, agg, 1))
                total[slots_ref[t, 2 * pair + 1, k]] += jnp.where(low, pltpu.roll(even, agg, 1), odd)

    @pl.loop(0, count // GROUP)
    def _(g):
        for i in range(GROUP):
            block(g * GROUP + i)

    @pl.loop(0, out_ref.shape[0] // 8)
    def _(g):
        some = pl.ds(pl.multiple_of(g * 8, 8), 8)
        out_ref[some] = functools.reduce(lambda p, q: p + q, [total[some] for total in totals]).astype(BF16)


def local_terms(a_blocks, a_rows, a_cols, slots, row_panel, col_panel, slot_count):
    count = a_blocks.shape[0]
    panel_rows, node, width = row_panel.shape
    agg = width // KP
    vmem, smem = pl.BlockSpec(memory_space=pltpu.VMEM), pl.BlockSpec(memory_space=pltpu.SMEM)
    return pl.pallas_call(
        functools.partial(terms_kernel),
        out_shape=jax.ShapeDtypeStruct((slot_count, agg // 2, 2 * agg), BF16),
        in_specs=[smem, smem, smem, vmem, vmem, vmem],
        out_specs=vmem,
        scratch_shapes=[pltpu.VMEM((panel_rows, width, node), BF16), pltpu.VMEM((count, width, node), BF16)]
        + [pltpu.VMEM((slot_count, agg // 2, 2 * agg), F32)] * 2,
        compiler_params=pltpu.CompilerParams(vmem_limit_bytes=36 << 20),
        name="terms",
    )(a_rows, a_cols, jnp.transpose(slots, (1, 2, 0)), a_blocks, row_panel, col_panel)


def sums_kernel(ncol, part_ref, out_ref, landed, own_sem, send_sem, recv_sem):
    r, c = lax.axis_index("row"), lax.axis_index("col")
    share = out_ref.shape[0]
    barrier = pltpu.get_barrier_semaphore()
    for d in range(1, ncol):
        pl.semaphore_signal(barrier, inc=1, device_id=(r, (c + d) % ncol), device_id_type=MESH)
    pl.semaphore_wait(barrier, ncol - 1)

    def copy(d):
        target = (c + d) % ncol
        return pltpu.make_async_remote_copy(
            src_ref=part_ref.at[pl.ds(target * share, share)],
            dst_ref=landed.at[d],
            send_sem=send_sem.at[d],
            recv_sem=recv_sem.at[d],
            device_id=(r, target),
            device_id_type=MESH,
        )

    for d in range(1, ncol):
        copy(d).start()
    mine = pltpu.make_async_copy(part_ref.at[pl.ds(c * share, share)], landed.at[0], own_sem)
    mine.start()
    mine.wait()
    for d in range(1, ncol):
        copy(d).wait_recv()
    for d in range(1, ncol):
        copy(d).wait_send()
    rows, lanes = landed.shape[2:]
    total = landed[0].astype(F32)
    for d in range(1, ncol):
        total = total + landed[d].astype(F32)
    for i in range(rows):
        out_ref[:, i * lanes : (i + 1) * lanes] = total[:, i, :].astype(BF16)


def sum_at_owner(partial, ncol):
    slots, rows, lanes = partial.shape
    share = slots // ncol
    vmem = pl.BlockSpec(memory_space=pltpu.VMEM)
    dma = pltpu.SemaphoreType.DMA
    return pl.pallas_call(
        functools.partial(sums_kernel, ncol),
        out_shape=jax.ShapeDtypeStruct((share, rows * lanes), BF16),
        in_specs=[vmem],
        out_specs=vmem,
        scratch_shapes=[
            pltpu.VMEM((ncol, share, rows, lanes), BF16),
            dma,
            dma((ncol,)),
            dma((ncol,)),
        ],
        compiler_params=pltpu.CompilerParams(collective_id=1, has_side_effects=True, vmem_limit_bytes=16 << 20),
        name="sums",
    )(partial)


def on_device(dims, slot_count, a_blocks, a_rows, a_cols, p_blocks, coarse_slot):
    ncol = dims[1] * dims[2]
    row_panel, col_panel = panels(p_blocks, dims)
    partial = local_terms(
        a_blocks[0, 0], a_rows[0, 0], a_cols[0, 0], coarse_slot[0, 0], row_panel, col_panel, slot_count
    )
    return sum_at_owner(partial, ncol)[None]


def solution(mesh, dims=(16, 4, 4), slot_count=128):
    placed = (
        P("row", "col", None, None, None),
        P("row", "col", None),
        P("row", "col", None),
        P(("row", "col"), None, None),
        P("row", "col", None, None, None),
    )
    return jax.shard_map(
        functools.partial(on_device, dims, slot_count),
        mesh=mesh,
        in_specs=placed,
        out_specs=P("row", "col", None),
        check_vma=False,
    )
```

```python
import functools

import jax
import jax.numpy as jnp
from jax import lax
from jax.experimental import pallas as pl
from jax.experimental.pallas import tpu as pltpu
from jax.sharding import PartitionSpec as P

MESH = pl.DeviceIdType.MESH
BF16, F32 = jnp.bfloat16, jnp.float32

HOP = 4
KP = 4
GROUP = 16
PARTS = 2


def gray(v):
    return v + v // 2 - 2 * ((v // 2) * (v % 2))


def panels_kernel(dims, p_ref, row_ref, col_ref, passing, own_sem, g_send, g_recv, r_send, r_recv, z_send, z_recv, a_send, a_recv, s_send, s_recv):
    nz, ny, nx = dims
    ncol = ny * nx
    r, c = lax.axis_index("row"), lax.axis_index("col")
    z, core = r // 2, r % 2
    y, x = c // nx, c % nx
    up, down = 2 * ((z + 1) % nz) + core, 2 * ((z + nz - 1) % nz) + core
    sibling = 2 * z + 1 - core
    base = core * 2 * ncol
    far = nz // 2
    steps_x = [gray(v) for v in range(1, nx)]
    steps_y = [gray(v) for v in range(1, ny)]

    def along_x(d):
        return y * nx + (x + d) % nx

    def along_y(d):
        return ((y + d) % ny) * nx + x

    barrier = pltpu.get_barrier_semaphore()
    peers = [(r, along_x(d)) for d in steps_x] + [(r, along_y(d)) for d in steps_y]
    peers += [(up, c), (down, c), (sibling, c)]
    for peer in peers:
        pl.semaphore_signal(barrier, inc=1, device_id=peer, device_id_type=MESH)
    pl.semaphore_wait(barrier, len(peers))

    def remote(src, dst, send, recv, device):
        return pltpu.make_async_remote_copy(
            src_ref=src, dst_ref=dst, send_sem=send, recv_sem=recv, device_id=device, device_id_type=MESH
        )

    root = x == z % nx
    plane = z // nx

    def gather_copy(x0):
        return remote(p_ref, passing.at[plane, x0], g_send, g_recv.at[x0], (r, y * nx + z % nx))

    part = p_ref.shape[1] // PARTS

    def z_copy(way, y1, x0, j):
        here = passing.at[y1, x0, j // PARTS, pl.ds(pl.multiple_of(j % PARTS * part, part), part)]
        return remote(here, here, z_send.at[way, y1, x0, j], z_recv.at[way, y1, x0, j], (up if way == 0 else down, c))

    def name(way, pos):
        o = pos if way == 0 else (nx - pos) % nx
        return (x + o) % nx, (o < nx // 2 if way == 0 else o >= nx // 2)

    def a_copy(y1, x0):
        rows = col_ref.at[pl.ds(base + 2 * (y * nx + x0), 2)]
        return remote(passing.at[y1, x0], rows, a_send.at[y1, x0], a_recv.at[y * nx + x0], (r, y1 * nx + x))

    def deliver(y1, x0):
        @pl.when(y1 != y)
        def _():
            a_copy(y1, x0).start()

        @pl.when(y1 == y)
        def _():
            rows = col_ref.at[pl.ds(base + 2 * (y * nx + x0), 2)]
            pltpu.make_async_copy(passing.at[y1, x0], rows, a_recv.at[y * nx + x0]).start()

    sends = []

    def give(src, piece, target):
        rows = row_ref.at[pl.ds(2 * piece, 2)]
        copy = remote(src, rows, r_send.at[len(sends)], r_recv.at[piece], (r, target))
        copy.start()
        sends.append(copy)

    def arrived(piece):
        rows = row_ref.at[pl.ds(2 * piece, 2)]
        remote(rows, rows, r_send.at[0], r_recv.at[piece], (r, c)).wait_recv()

    @pl.when(jnp.logical_not(root))
    def _():
        gather_copy(x).start()

    @pl.when(root)
    def _():
        copy = pltpu.make_async_copy(p_ref, passing.at[plane, x], own_sem.at[1])
        copy.start()
        copy.wait()
        for j in range(2 * PARTS):
            z_copy(0, plane, x, j).start()
            z_copy(1, plane, x, j).start()
        deliver(plane, x)

    mine = pltpu.make_async_copy(p_ref, row_ref.at[pl.ds(2 * c, 2)], own_sem.at[0])
    mine.start()
    for d in steps_y:
        give(p_ref, c, along_y(d))
    for d in steps_x:
        give(p_ref, c, along_x(d))

    @pl.when(root)
    def _():
        for pos in range(1, nx):
            a, b = name(0, pos)[0], name(1, pos)[0]
            if 2 * pos <= nx:
                gather_copy(a).wait_recv()
                if 2 * pos < nx:
                    gather_copy(b).wait_recv()
            for j in range(2 * PARTS):
                z_copy(0, plane, a, j).start()
                z_copy(1, plane, b, j).start()
            deliver(plane, a)

    for d in steps_y:
        piece = along_y(d)
        arrived(piece)
        for e in steps_x:
            give(row_ref.at[pl.ds(2 * piece, 2)], piece, along_x(e))

    near_up = (z - x + nz - 1) % nx + 1
    near_down = (x - z + nz - 1) % nx + 1
    feeds, parts = far // nx, 2 * PARTS
    chunks = nx * parts

    def chunk(way, feed, n):
        dist = (near_up if way == 0 else near_down) + nx * feed
        z0 = (z - dist + nz) % nz if way == 0 else (z + dist) % nz
        x0, opposite = name(way, n // parts)
        comes = (dist < far) | ((dist == far) & opposite)
        goes = (dist < far - 1) | ((dist == far - 1) & opposite)
        return z0 // nx, x0, n % parts, comes, goes

    def relay(way, feed, n):
        y1, x0, j, comes, goes = chunk(way, feed, n)

        @pl.when(comes)
        def _():
            z_copy(way, y1, x0, j).wait_recv()

            @pl.when(goes)
            def _():
                z_copy(way, y1, x0, j).start()

            @pl.when(j == parts - 1)
            def _():
                deliver(y1, x0)

    @pl.loop(0, chunks + HOP * (far - 1))
    def _(step):
        for feed in range(feeds):
            for way, near in ((0, near_up), (1, near_down)):
                n = step - HOP * (near + nx * feed - 1)

                @pl.when((n >= 0) & (n < chunks))
                def _():
                    relay(way, feed, n)

    def s_copy(c0):
        rows = col_ref.at[pl.ds(base + 2 * c0, 2)]
        return remote(rows, rows, s_send.at[c0], s_recv.at[c0], (sibling, c))

    @pl.loop(0, ncol)
    def _(i):
        c0 = (c + i) % ncol
        rows = col_ref.at[pl.ds(base + 2 * c0, 2)]
        remote(passing.at[0, 0], rows, a_send.at[0, 0], a_recv.at[c0], (r, c)).wait_recv()
        s_copy(c0).start()

    for u in range(ny):
        for v in range(1, nx):
            arrived(((y + u) % ny) * nx + (x + v) % nx)
    mine.wait()
    for copy in sends:
        copy.wait_send()

    @pl.when(jnp.logical_not(root))
    def _():
        gather_copy(x).wait_send()

    @pl.loop(0, nx)
    def _(x0):
        @pl.when(root)
        def _():
            for j in range(2 * PARTS):
                z_copy(0, plane, x0, j).wait_send()
                z_copy(1, plane, x0, j).wait_send()

        for y1 in range(ny):
            @pl.when(y1 != y)
            def _():
                a_copy(y1, x0).wait_send()

    @pl.loop(0, chunks)
    def _(n):
        for feed in range(feeds):
            for way in (0, 1):
                y1, x0, j, comes, goes = chunk(way, feed, n)

                @pl.when(comes & goes)
                def _():
                    z_copy(way, y1, x0, j).wait_send()

    @pl.loop(0, ncol)
    def _(c0):
        s_copy(c0).wait_send()
        s_copy(c0).wait_recv()


def panels(p_blocks, dims):
    nz, ny, nx = dims
    ncol = ny * nx
    _, node, width = p_blocks.shape
    vmem = pl.BlockSpec(memory_space=pltpu.VMEM)
    dma = pltpu.SemaphoreType.DMA
    return pl.pallas_call(
        functools.partial(panels_kernel, dims),
        out_shape=(
            jax.ShapeDtypeStruct((2 * ncol, node, width), BF16),
            jax.ShapeDtypeStruct((4 * ncol, node, width), BF16),
        ),
        in_specs=[vmem],
        out_specs=(vmem, vmem),
        scratch_shapes=[
            pltpu.VMEM((ny, nx, 2, node, width), BF16),
            dma((2,)),
            dma,
            dma((nx,)),
            dma((ncol - 1,)),
            dma((ncol,)),
            dma((2, ny, nx, 2 * PARTS)),
            dma((2, ny, nx, 2 * PARTS)),
            dma((ny, nx)),
            dma((ncol,)),
            dma((ncol,)),
            dma((ncol,)),
        ],
        compiler_params=pltpu.CompilerParams(collective_id=0, has_side_effects=True, vmem_limit_bytes=16 << 20),
        name="panels",
    )(p_blocks)


def terms_kernel(rows_ref, cols_ref, slots_ref, a_ref, row_ref, col_ref, out_ref, turned, left_ref, *totals):
    count, width, node = left_ref.shape
    panel_rows = row_ref.shape[0]
    agg = width // KP
    half = agg // 2

    @pl.loop(0, out_ref.shape[0] // 8)
    def _(g):
        some = pl.ds(pl.multiple_of(g * 8, 8), 8)
        for total in totals:
            total[some] = jnp.zeros((8, *total.shape[1:]), F32)

    to = lax.broadcasted_iota(jnp.int32, (width, width), 0)
    at = lax.broadcasted_iota(jnp.int32, (width, width), 1)
    inner = to % agg
    source = to - inner + 2 * (inner % half) + inner // half
    pick = jnp.where(at == source, 1.0, 0.0).astype(BF16)

    @pl.loop(0, panel_rows // 8)
    def _(g):
        for i in range(8):
            turned[g * 8 + i] = lax.dot_general(
                pick, row_ref[g * 8 + i], (((1,), (1,)), ((), ())), preferred_element_type=F32
            ).astype(BF16)

    @pl.loop(0, count // GROUP)
    def _(g):
        for i in range(GROUP):
            k = g * GROUP + i
            left_ref[k] = jnp.dot(turned[rows_ref[k]], a_ref[k], preferred_element_type=F32).astype(BF16)

    low = lax.broadcasted_iota(jnp.int32, (half, 2 * agg), 1) < agg

    def block(k):
        term = jnp.dot(left_ref[k], col_ref[cols_ref[k]], preferred_element_type=F32)
        for pair in range(KP // 2):
            lanes = slice(pair * 2 * agg, (pair + 1) * 2 * agg)
            for t in range(KP):
                even = term[t * agg : t * agg + half, lanes]
                odd = term[t * agg + half : (t + 1) * agg, lanes]
                total = totals[t % len(totals)]
                total[slots_ref[t, 2 * pair, k]] += jnp.where(low, even, pltpu.roll(odd, agg, 1))
                total[slots_ref[t, 2 * pair + 1, k]] += jnp.where(low, pltpu.roll(even, agg, 1), odd)

    @pl.loop(0, count // GROUP)
    def _(g):
        for i in range(GROUP):
            block(g * GROUP + i)

    @pl.loop(0, out_ref.shape[0] // 8)
    def _(g):
        some = pl.ds(pl.multiple_of(g * 8, 8), 8)
        out_ref[some] = functools.reduce(lambda p, q: p + q, [total[some] for total in totals]).astype(BF16)


def local_terms(a_blocks, a_rows, a_cols, slots, row_panel, col_panel, slot_count):
    count = a_blocks.shape[0]
    panel_rows, node, width = row_panel.shape
    agg = width // KP
    vmem, smem = pl.BlockSpec(memory_space=pltpu.VMEM), pl.BlockSpec(memory_space=pltpu.SMEM)
    return pl.pallas_call(
        functools.partial(terms_kernel),
        out_shape=jax.ShapeDtypeStruct((slot_count, agg // 2, 2 * agg), BF16),
        in_specs=[smem, smem, smem, vmem, vmem, vmem],
        out_specs=vmem,
        scratch_shapes=[pltpu.VMEM((panel_rows, width, node), BF16), pltpu.VMEM((count, width, node), BF16)]
        + [pltpu.VMEM((slot_count, agg // 2, 2 * agg), F32)] * 2,
        compiler_params=pltpu.CompilerParams(vmem_limit_bytes=36 << 20),
        name="terms",
    )(a_rows, a_cols, jnp.transpose(slots, (1, 2, 0)), a_blocks, row_panel, col_panel)


def sums_kernel(dims, part_ref, out_ref, landed, middle, last, send_sem, recv_sem, send_last, recv_last):
    _, ny, nx = dims
    r, c = lax.axis_index("row"), lax.axis_index("col")
    y, x = c // nx, c % nx
    half = out_ref.shape[0] // 2
    steps_x = [gray(v) for v in range(1, nx)]
    steps_y = [gray(v) for v in range(1, ny)]
    first, second = pl.ds(0, half), pl.ds(half, half)

    barrier = pltpu.get_barrier_semaphore()
    peers = [(r, y * nx + (x + d) % nx) for d in steps_x] + [(r, (y + d) % ny * nx + x) for d in steps_y]
    for peer in peers:
        pl.semaphore_signal(barrier, inc=1, device_id=peer, device_id_type=MESH)
    pl.semaphore_wait(barrier, len(peers))

    def remote(src, dst, send, recv, target):
        return pltpu.make_async_remote_copy(
            src_ref=src, dst_ref=dst, send_sem=send, recv_sem=recv, device_id=(r, target), device_id_type=MESH
        )

    def copy(way, d):
        if way == 0:
            x1 = (x + d) % nx
            src, target = part_ref.at[:, x1, first], y * nx + x1
        else:
            y1 = (y + d) % ny
            src, target = part_ref.at[y1, :, second], y1 * nx + x
        return remote(src, landed.at[way, d], send_sem.at[way, d], recv_sem.at[way, d], target)

    def copy_last(way, d):
        i = (y + d) % ny if way == 0 else (x + d) % nx
        target = i * nx + x if way == 0 else y * nx + i
        return remote(middle.at[way, d], last.at[way, d], send_last.at[way, d], recv_last.at[way, d], target)

    steps = (steps_x, steps_y)
    for dx, dy in zip(*steps):
        copy(0, dx).start()
        copy(1, dy).start()
    for way in (0, 1):
        for d in steps[way]:
            copy(way, d).wait_recv()

    def summed(way, i):
        own = part_ref[i, x, first] if way == 0 else part_ref[y, i, second]
        total = own.astype(F32)
        for d in steps[way]:
            total = total + landed[way, d, i].astype(F32)
        return total

    for dy, dx in zip(steps_y, steps_x):
        middle[0, dy] = summed(0, (y + dy) % ny)
        copy_last(0, dy).start()
        middle[1, dx] = summed(1, (x + dx) % nx)
        copy_last(1, dx).start()
    totals = [summed(0, y), summed(1, x)]
    for way in (0, 1):
        for d in steps[1 - way]:
            copy_last(way, d).wait_recv()
            totals[way] = totals[way] + last[way, d]
    total = jnp.concatenate(totals, axis=0)
    rows, lanes = total.shape[1:]
    for i in range(rows):
        out_ref[:, i * lanes : (i + 1) * lanes] = total[:, i, :].astype(BF16)
    for way in (0, 1):
        for d in steps[way]:
            copy(way, d).wait_send()
        for d in steps[1 - way]:
            copy_last(way, d).wait_send()


def sum_at_owner(partial, dims):
    _, ny, nx = dims
    assert ny == nx
    slots, rows, lanes = partial.shape
    share = slots // (ny * nx)
    half = (share // 2, rows, lanes)
    vmem = pl.BlockSpec(memory_space=pltpu.VMEM)
    dma = pltpu.SemaphoreType.DMA
    return pl.pallas_call(
        functools.partial(sums_kernel, dims),
        out_shape=jax.ShapeDtypeStruct((share, rows * lanes), BF16),
        in_specs=[vmem],
        out_specs=vmem,
        scratch_shapes=[
            pltpu.VMEM((2, nx, nx, *half), BF16),
            pltpu.VMEM((2, nx, *half), F32),
            pltpu.VMEM((2, nx, *half), F32),
            dma((2, nx)),
            dma((2, nx)),
            dma((2, nx)),
            dma((2, nx)),
        ],
        compiler_params=pltpu.CompilerParams(collective_id=1, has_side_effects=True, vmem_limit_bytes=16 << 20),
        name="sums",
    )(partial.reshape(ny, nx, share, rows, lanes))


def on_device(dims, slot_count, a_blocks, a_rows, a_cols, p_blocks, coarse_slot):
    row_panel, col_panel = panels(p_blocks, dims)
    partial = local_terms(
        a_blocks[0, 0], a_rows[0, 0], a_cols[0, 0], coarse_slot[0, 0], row_panel, col_panel, slot_count
    )
    return sum_at_owner(partial, dims)[None]


def solution(mesh, dims=(16, 4, 4), slot_count=128):
    placed = (
        P("row", "col", None, None, None),
        P("row", "col", None),
        P("row", "col", None),
        P(("row", "col"), None, None),
        P("row", "col", None, None, None),
    )
    return jax.shard_map(
        functools.partial(on_device, dims, slot_count),
        mesh=mesh,
        in_specs=placed,
        out_specs=P("row", "col", None),
        check_vma=False,
    )
```

```python
import functools

import jax
import jax.numpy as jnp
from jax import lax
from jax.experimental import pallas as pl
from jax.experimental.pallas import tpu as pltpu
from jax.sharding import PartitionSpec as P

MESH = pl.DeviceIdType.MESH
BF16, F32 = jnp.bfloat16, jnp.float32

HOP = 4
KP = 4
GROUP = 16
PARTS = 2


def gray(v):
    return v + v // 2 - 2 * ((v // 2) * (v % 2))


def panels_kernel(dims, p_ref, row_ref, col_ref, passing, own_sem, g_send, g_recv, r_send, r_recv, z_send, z_recv, a_send, a_recv, s_send, s_recv):
    nz, ny, nx = dims
    ncol = ny * nx
    r, c = lax.axis_index("row"), lax.axis_index("col")
    z, core = r // 2, r % 2
    y, x = c // nx, c % nx
    up, down = 2 * ((z + 1) % nz) + core, 2 * ((z + nz - 1) % nz) + core
    sibling = 2 * z + 1 - core
    base = core * 2 * ncol
    far = nz // 2
    steps_x = [gray(v) for v in range(1, nx)]
    steps_y = [gray(v) for v in range(1, ny)]

    def along_x(d):
        return y * nx + (x + d) % nx

    def along_y(d):
        return ((y + d) % ny) * nx + x

    barrier = pltpu.get_barrier_semaphore()
    peers = [(r, along_x(d)) for d in steps_x] + [(r, along_y(d)) for d in steps_y]
    peers += [(up, c), (down, c), (sibling, c)]
    for peer in peers:
        pl.semaphore_signal(barrier, inc=1, device_id=peer, device_id_type=MESH)
    pl.semaphore_wait(barrier, len(peers))

    def remote(src, dst, send, recv, device):
        return pltpu.make_async_remote_copy(
            src_ref=src, dst_ref=dst, send_sem=send, recv_sem=recv, device_id=device, device_id_type=MESH
        )

    root = x == z % nx
    plane = z // nx

    def gather_copy(x0):
        return remote(p_ref, passing.at[plane, x0], g_send, g_recv.at[x0], (r, y * nx + z % nx))

    part = p_ref.shape[1] // PARTS

    def z_copy(way, y1, x0, j):
        here = passing.at[y1, x0, j // PARTS, pl.ds(pl.multiple_of(j % PARTS * part, part), part)]
        return remote(here, here, z_send.at[way, y1, x0, j], z_recv.at[way, y1, x0, j], (up if way == 0 else down, c))

    def name(way, pos):
        o = pos if way == 0 else (nx - pos) % nx
        return (x + o) % nx, (o < nx // 2 if way == 0 else o >= nx // 2)

    def a_copy(y1, x0):
        rows = col_ref.at[pl.ds(base + 2 * (y * nx + x0), 2)]
        return remote(passing.at[y1, x0], rows, a_send.at[y1, x0], a_recv.at[y * nx + x0], (r, y1 * nx + x))

    def deliver(y1, x0):
        @pl.when(y1 != y)
        def _():
            a_copy(y1, x0).start()

        @pl.when(y1 == y)
        def _():
            rows = col_ref.at[pl.ds(base + 2 * (y * nx + x0), 2)]
            pltpu.make_async_copy(passing.at[y1, x0], rows, a_recv.at[y * nx + x0]).start()

    sends = []

    def give(src, piece, target):
        rows = row_ref.at[pl.ds(2 * piece, 2)]
        copy = remote(src, rows, r_send.at[len(sends)], r_recv.at[piece], (r, target))
        copy.start()
        sends.append(copy)

    def arrived(piece):
        rows = row_ref.at[pl.ds(2 * piece, 2)]
        remote(rows, rows, r_send.at[0], r_recv.at[piece], (r, c)).wait_recv()

    @pl.when(jnp.logical_not(root))
    def _():
        gather_copy(x).start()

    @pl.when(root)
    def _():
        copy = pltpu.make_async_copy(p_ref, passing.at[plane, x], own_sem.at[1])
        copy.start()
        copy.wait()
        for j in range(2 * PARTS):
            z_copy(0, plane, x, j).start()
            z_copy(1, plane, x, j).start()
        deliver(plane, x)

    mine = pltpu.make_async_copy(p_ref, row_ref.at[pl.ds(2 * c, 2)], own_sem.at[0])
    mine.start()
    for d in steps_y:
        give(p_ref, c, along_y(d))
    for d in steps_x:
        give(p_ref, c, along_x(d))

    @pl.when(root)
    def _():
        for pos in range(1, nx):
            a, b = name(0, pos)[0], name(1, pos)[0]
            if 2 * pos <= nx:
                gather_copy(a).wait_recv()
                if 2 * pos < nx:
                    gather_copy(b).wait_recv()
            for j in range(2 * PARTS):
                z_copy(0, plane, a, j).start()
                z_copy(1, plane, b, j).start()
            deliver(plane, a)

    for d in steps_y:
        piece = along_y(d)
        arrived(piece)
        for e in steps_x:
            give(row_ref.at[pl.ds(2 * piece, 2)], piece, along_x(e))

    near_up = (z - x + nz - 1) % nx + 1
    near_down = (x - z + nz - 1) % nx + 1
    feeds, parts = far // nx, 2 * PARTS
    chunks = nx * parts

    def chunk(way, feed, n):
        dist = (near_up if way == 0 else near_down) + nx * feed
        z0 = (z - dist + nz) % nz if way == 0 else (z + dist) % nz
        x0, opposite = name(way, n // parts)
        comes = (dist < far) | ((dist == far) & opposite)
        goes = (dist < far - 1) | ((dist == far - 1) & opposite)
        return z0 // nx, x0, n % parts, comes, goes

    def relay(way, feed, n):
        y1, x0, j, comes, goes = chunk(way, feed, n)

        @pl.when(comes)
        def _():
            z_copy(way, y1, x0, j).wait_recv()

            @pl.when(goes)
            def _():
                z_copy(way, y1, x0, j).start()

            @pl.when(j == parts - 1)
            def _():
                deliver(y1, x0)

    @pl.loop(0, chunks + HOP * (far - 1))
    def _(step):
        for feed in range(feeds):
            for way, near in ((0, near_up), (1, near_down)):
                n = step - HOP * (near + nx * feed - 1)

                @pl.when((n >= 0) & (n < chunks))
                def _():
                    relay(way, feed, n)

    def s_copy(c0):
        rows = col_ref.at[pl.ds(base + 2 * c0, 2)]
        return remote(rows, rows, s_send.at[c0], s_recv.at[c0], (sibling, c))

    @pl.loop(0, ncol)
    def _(i):
        c0 = (c + i) % ncol
        rows = col_ref.at[pl.ds(base + 2 * c0, 2)]
        remote(passing.at[0, 0], rows, a_send.at[0, 0], a_recv.at[c0], (r, c)).wait_recv()
        s_copy(c0).start()

    for u in range(ny):
        for v in range(1, nx):
            arrived(((y + u) % ny) * nx + (x + v) % nx)
    mine.wait()
    for copy in sends:
        copy.wait_send()

    @pl.when(jnp.logical_not(root))
    def _():
        gather_copy(x).wait_send()

    @pl.loop(0, nx)
    def _(x0):
        @pl.when(root)
        def _():
            for j in range(2 * PARTS):
                z_copy(0, plane, x0, j).wait_send()
                z_copy(1, plane, x0, j).wait_send()

        for y1 in range(ny):
            @pl.when(y1 != y)
            def _():
                a_copy(y1, x0).wait_send()

    @pl.loop(0, chunks)
    def _(n):
        for feed in range(feeds):
            for way in (0, 1):
                y1, x0, j, comes, goes = chunk(way, feed, n)

                @pl.when(comes & goes)
                def _():
                    z_copy(way, y1, x0, j).wait_send()

    @pl.loop(0, ncol)
    def _(c0):
        s_copy(c0).wait_send()
        s_copy(c0).wait_recv()


def panels(p_blocks, dims):
    nz, ny, nx = dims
    ncol = ny * nx
    _, node, width = p_blocks.shape
    vmem = pl.BlockSpec(memory_space=pltpu.VMEM)
    dma = pltpu.SemaphoreType.DMA
    return pl.pallas_call(
        functools.partial(panels_kernel, dims),
        out_shape=(
            jax.ShapeDtypeStruct((2 * ncol, node, width), BF16),
            jax.ShapeDtypeStruct((4 * ncol, node, width), BF16),
        ),
        in_specs=[pl.BlockSpec(memory_space=pltpu.HBM)],
        out_specs=(vmem, vmem),
        scratch_shapes=[
            pltpu.VMEM((ny, nx, 2, node, width), BF16),
            dma((2,)),
            dma,
            dma((nx,)),
            dma((ncol - 1,)),
            dma((ncol,)),
            dma((2, ny, nx, 2 * PARTS)),
            dma((2, ny, nx, 2 * PARTS)),
            dma((ny, nx)),
            dma((ncol,)),
            dma((ncol,)),
            dma((ncol,)),
        ],
        compiler_params=pltpu.CompilerParams(collective_id=0, has_side_effects=True, vmem_limit_bytes=16 << 20),
        name="panels",
    )(pltpu.with_memory_space_constraint(p_blocks, pltpu.HBM))


def terms_kernel(
    rows_hbm, cols_hbm, slots_hbm, a_hbm, row_ref, col_ref, out_ref, sem, rows_ref, cols_ref, slots_ref, a_ref, turned, left_ref, *totals
):
    count, width, node = left_ref.shape
    panel_rows = row_ref.shape[0]
    fetches = [
        pltpu.make_async_copy(src, dst, sem.at[i])
        for i, (src, dst) in enumerate(
            ((a_hbm, a_ref), (rows_hbm, rows_ref), (cols_hbm, cols_ref), (slots_hbm, slots_ref))
        )
    ]
    for fetch in fetches:
        fetch.start()
    agg = width // KP
    half = agg // 2

    @pl.loop(0, out_ref.shape[0] // 8)
    def _(g):
        some = pl.ds(pl.multiple_of(g * 8, 8), 8)
        for total in totals:
            total[some] = jnp.zeros((8, *total.shape[1:]), F32)

    to = lax.broadcasted_iota(jnp.int32, (width, width), 0)
    at = lax.broadcasted_iota(jnp.int32, (width, width), 1)
    inner = to % agg
    source = to - inner + 2 * (inner % half) + inner // half
    pick = jnp.where(at == source, 1.0, 0.0).astype(BF16)

    @pl.loop(0, panel_rows // 8)
    def _(g):
        for i in range(8):
            turned[g * 8 + i] = lax.dot_general(
                pick, row_ref[g * 8 + i], (((1,), (1,)), ((), ())), preferred_element_type=F32
            ).astype(BF16)

    for fetch in fetches:
        fetch.wait()

    @pl.loop(0, count // GROUP)
    def _(g):
        for i in range(GROUP):
            k = g * GROUP + i
            left_ref[k] = jnp.dot(turned[rows_ref[k]], a_ref[k], preferred_element_type=F32).astype(BF16)

    low = lax.broadcasted_iota(jnp.int32, (half, 2 * agg), 1) < agg

    def block(k):
        term = jnp.dot(left_ref[k], col_ref[cols_ref[k]], preferred_element_type=F32)
        for pair in range(KP // 2):
            lanes = slice(pair * 2 * agg, (pair + 1) * 2 * agg)
            for t in range(KP):
                even = term[t * agg : t * agg + half, lanes]
                odd = term[t * agg + half : (t + 1) * agg, lanes]
                total = totals[t % len(totals)]
                total[slots_ref[t, 2 * pair, k]] += jnp.where(low, even, pltpu.roll(odd, agg, 1))
                total[slots_ref[t, 2 * pair + 1, k]] += jnp.where(low, pltpu.roll(even, agg, 1), odd)

    @pl.loop(0, count // GROUP)
    def _(g):
        for i in range(GROUP):
            block(g * GROUP + i)

    @pl.loop(0, out_ref.shape[0] // 8)
    def _(g):
        some = pl.ds(pl.multiple_of(g * 8, 8), 8)
        out_ref[some] = functools.reduce(lambda p, q: p + q, [total[some] for total in totals]).astype(BF16)


def local_terms(a_blocks, a_rows, a_cols, slots, row_panel, col_panel, slot_count):
    count = a_blocks.shape[0]
    panel_rows, node, width = row_panel.shape
    agg = width // KP
    slots = jnp.transpose(slots, (1, 2, 0))
    vmem, hbm = pl.BlockSpec(memory_space=pltpu.VMEM), pl.BlockSpec(memory_space=pltpu.HBM)
    return pl.pallas_call(
        functools.partial(terms_kernel),
        out_shape=jax.ShapeDtypeStruct((slot_count, agg // 2, 2 * agg), BF16),
        in_specs=[hbm, hbm, hbm, hbm, vmem, vmem],
        out_specs=vmem,
        scratch_shapes=[pltpu.SemaphoreType.DMA((4,))]
        + [pltpu.SMEM(ids.shape, jnp.int32) for ids in (a_rows, a_cols, slots)]
        + [pltpu.VMEM(a_blocks.shape, BF16)]
        + [pltpu.VMEM((panel_rows, width, node), BF16), pltpu.VMEM((count, width, node), BF16)]
        + [pltpu.VMEM((slot_count, agg // 2, 2 * agg), F32)] * 2,
        compiler_params=pltpu.CompilerParams(vmem_limit_bytes=36 << 20),
        name="terms",
    )(*(pltpu.with_memory_space_constraint(v, pltpu.HBM) for v in (a_rows, a_cols, slots, a_blocks)), row_panel, col_panel)


def sums_kernel(dims, part_ref, out_ref, landed, middle, last, send_sem, recv_sem, send_last, recv_last):
    _, ny, nx = dims
    r, c = lax.axis_index("row"), lax.axis_index("col")
    y, x = c // nx, c % nx
    half = out_ref.shape[0] // 2
    steps_x = [gray(v) for v in range(1, nx)]
    steps_y = [gray(v) for v in range(1, ny)]
    first, second = pl.ds(0, half), pl.ds(half, half)

    barrier = pltpu.get_barrier_semaphore()
    peers = [(r, y * nx + (x + d) % nx) for d in steps_x] + [(r, (y + d) % ny * nx + x) for d in steps_y]
    for peer in peers:
        pl.semaphore_signal(barrier, inc=1, device_id=peer, device_id_type=MESH)
    pl.semaphore_wait(barrier, len(peers))

    def remote(src, dst, send, recv, target):
        return pltpu.make_async_remote_copy(
            src_ref=src, dst_ref=dst, send_sem=send, recv_sem=recv, device_id=(r, target), device_id_type=MESH
        )

    def copy(way, d):
        if way == 0:
            x1 = (x + d) % nx
            src, target = part_ref.at[:, x1, first], y * nx + x1
        else:
            y1 = (y + d) % ny
            src, target = part_ref.at[y1, :, second], y1 * nx + x
        return remote(src, landed.at[way, d], send_sem.at[way, d], recv_sem.at[way, d], target)

    def copy_last(way, d):
        i = (y + d) % ny if way == 0 else (x + d) % nx
        target = i * nx + x if way == 0 else y * nx + i
        return remote(middle.at[way, d], last.at[way, d], send_last.at[way, d], recv_last.at[way, d], target)

    steps = (steps_x, steps_y)
    for dx, dy in zip(*steps):
        copy(0, dx).start()
        copy(1, dy).start()
    for way in (0, 1):
        for d in steps[way]:
            copy(way, d).wait_recv()

    def summed(way, i):
        own = part_ref[i, x, first] if way == 0 else part_ref[y, i, second]
        total = own.astype(F32)
        for d in steps[way]:
            total = total + landed[way, d, i].astype(F32)
        return total

    for dy, dx in zip(steps_y, steps_x):
        middle[0, dy] = summed(0, (y + dy) % ny)
        copy_last(0, dy).start()
        middle[1, dx] = summed(1, (x + dx) % nx)
        copy_last(1, dx).start()
    totals = [summed(0, y), summed(1, x)]
    for way in (0, 1):
        for d in steps[1 - way]:
            copy_last(way, d).wait_recv()
            totals[way] = totals[way] + last[way, d]
    total = jnp.concatenate(totals, axis=0)
    rows, lanes = total.shape[1:]
    for i in range(rows):
        out_ref[:, i * lanes : (i + 1) * lanes] = total[:, i, :].astype(BF16)
    for way in (0, 1):
        for d in steps[way]:
            copy(way, d).wait_send()
        for d in steps[1 - way]:
            copy_last(way, d).wait_send()


def sum_at_owner(partial, dims):
    _, ny, nx = dims
    assert ny == nx
    slots, rows, lanes = partial.shape
    share = slots // (ny * nx)
    half = (share // 2, rows, lanes)
    vmem = pl.BlockSpec(memory_space=pltpu.VMEM)
    dma = pltpu.SemaphoreType.DMA
    return pl.pallas_call(
        functools.partial(sums_kernel, dims),
        out_shape=jax.ShapeDtypeStruct((share, rows * lanes), BF16),
        in_specs=[vmem],
        out_specs=vmem,
        scratch_shapes=[
            pltpu.VMEM((2, nx, nx, *half), BF16),
            pltpu.VMEM((2, nx, *half), F32),
            pltpu.VMEM((2, nx, *half), F32),
            dma((2, nx)),
            dma((2, nx)),
            dma((2, nx)),
            dma((2, nx)),
        ],
        compiler_params=pltpu.CompilerParams(collective_id=1, has_side_effects=True, vmem_limit_bytes=16 << 20),
        name="sums",
    )(partial.reshape(ny, nx, share, rows, lanes))


def on_device(dims, slot_count, a_blocks, a_rows, a_cols, p_blocks, coarse_slot):
    row_panel, col_panel = panels(p_blocks, dims)
    partial = local_terms(
        a_blocks[0, 0], a_rows[0, 0], a_cols[0, 0], coarse_slot[0, 0], row_panel, col_panel, slot_count
    )
    return sum_at_owner(partial, dims)[None]


def solution(mesh, dims=(16, 4, 4), slot_count=128):
    placed = (
        P("row", "col", None, None, None),
        P("row", "col", None),
        P("row", "col", None),
        P(("row", "col"), None, None),
        P("row", "col", None, None, None),
    )
    return jax.shard_map(
        functools.partial(on_device, dims, slot_count),
        mesh=mesh,
        in_specs=placed,
        out_specs=P("row", "col", None),
        check_vma=False,
    )
```

```python
import functools

import jax
import jax.numpy as jnp
from jax import lax
from jax.experimental import pallas as pl
from jax.experimental.pallas import tpu as pltpu
from jax.sharding import PartitionSpec as P

MESH = pl.DeviceIdType.MESH
BF16, F32 = jnp.bfloat16, jnp.float32

HOP = 4
KP = 4
GROUP = 24
PARTS = 2


def gray(v):
    return v + v // 2 - 2 * ((v // 2) * (v % 2))


def panels_kernel(
    dims, rows_hbm, a_hbm, p_ref, left_ref, col_ref, rows_ref, a_ref, row_ref, turned, passing, own_sem, g_send, g_recv, r_send, r_recv, z_send, z_recv, a_send, a_recv, s_send, s_recv):
    nz, ny, nx = dims
    ncol = ny * nx
    r, c = lax.axis_index("row"), lax.axis_index("col")
    z, core = r // 2, r % 2
    y, x = c // nx, c % nx
    up, down = 2 * ((z + 1) % nz) + core, 2 * ((z + nz - 1) % nz) + core
    sibling = 2 * z + 1 - core
    base = core * 2 * ncol
    far = nz // 2
    steps_x = [gray(v) for v in range(1, nx)]
    steps_y = [gray(v) for v in range(1, ny)]

    def along_x(d):
        return y * nx + (x + d) % nx

    def along_y(d):
        return ((y + d) % ny) * nx + x

    barrier = pltpu.get_barrier_semaphore()
    peers = [(r, along_x(d)) for d in steps_x] + [(r, along_y(d)) for d in steps_y]
    peers += [(up, c), (down, c), (sibling, c)]
    for peer in peers:
        pl.semaphore_signal(barrier, inc=1, device_id=peer, device_id_type=MESH)
    pl.semaphore_wait(barrier, len(peers))

    def remote(src, dst, send, recv, device):
        return pltpu.make_async_remote_copy(
            src_ref=src, dst_ref=dst, send_sem=send, recv_sem=recv, device_id=device, device_id_type=MESH
        )

    root = x == z % nx
    plane = z // nx

    def gather_copy(x0):
        return remote(p_ref, passing.at[plane, x0], g_send, g_recv.at[x0], (r, y * nx + z % nx))

    part = p_ref.shape[1] // PARTS

    def z_copy(way, y1, x0, j):
        here = passing.at[y1, x0, j // PARTS, pl.ds(pl.multiple_of(j % PARTS * part, part), part)]
        return remote(here, here, z_send.at[way, y1, x0, j], z_recv.at[way, y1, x0, j], (up if way == 0 else down, c))

    def name(way, pos):
        o = pos if way == 0 else (nx - pos) % nx
        return (x + o) % nx, (o < nx // 2 if way == 0 else o >= nx // 2)

    def a_copy(y1, x0):
        rows = col_ref.at[pl.ds(base + 2 * (y * nx + x0), 2)]
        return remote(passing.at[y1, x0], rows, a_send.at[y1, x0], a_recv.at[y * nx + x0], (r, y1 * nx + x))

    def deliver(y1, x0):
        @pl.when(y1 != y)
        def _():
            a_copy(y1, x0).start()

        @pl.when(y1 == y)
        def _():
            rows = col_ref.at[pl.ds(base + 2 * (y * nx + x0), 2)]
            pltpu.make_async_copy(passing.at[y1, x0], rows, a_recv.at[y * nx + x0]).start()

    sends = []

    def give(src, piece, target):
        rows = row_ref.at[pl.ds(2 * piece, 2)]
        copy = remote(src, rows, r_send.at[len(sends)], r_recv.at[piece], (r, target))
        copy.start()
        sends.append(copy)

    def arrived(piece):
        rows = row_ref.at[pl.ds(2 * piece, 2)]
        remote(rows, rows, r_send.at[0], r_recv.at[piece], (r, c)).wait_recv()

    @pl.when(jnp.logical_not(root))
    def _():
        gather_copy(x).start()

    @pl.when(root)
    def _():
        copy = pltpu.make_async_copy(p_ref, passing.at[plane, x], own_sem.at[1])
        copy.start()
        copy.wait()
        for j in range(2 * PARTS):
            z_copy(0, plane, x, j).start()
            z_copy(1, plane, x, j).start()
        deliver(plane, x)

    fetches = [
        pltpu.make_async_copy(rows_hbm, rows_ref, own_sem.at[2]),
        pltpu.make_async_copy(a_hbm, a_ref, own_sem.at[3]),
    ]
    for fetch in fetches:
        fetch.start()
    mine = pltpu.make_async_copy(p_ref, row_ref.at[pl.ds(2 * c, 2)], own_sem.at[0])
    mine.start()
    for d in steps_y:
        give(p_ref, c, along_y(d))
    for d in steps_x:
        give(p_ref, c, along_x(d))

    @pl.when(root)
    def _():
        for pos in range(1, nx):
            a, b = name(0, pos)[0], name(1, pos)[0]
            if 2 * pos <= nx:
                gather_copy(a).wait_recv()
                if 2 * pos < nx:
                    gather_copy(b).wait_recv()
            for j in range(2 * PARTS):
                z_copy(0, plane, a, j).start()
                z_copy(1, plane, b, j).start()
            deliver(plane, a)

    for d in steps_y:
        piece = along_y(d)
        arrived(piece)
        for e in steps_x:
            give(row_ref.at[pl.ds(2 * piece, 2)], piece, along_x(e))

    near_up = (z - x + nz - 1) % nx + 1
    near_down = (x - z + nz - 1) % nx + 1
    feeds, parts = far // nx, 2 * PARTS
    chunks = nx * parts

    def chunk(way, feed, n):
        dist = (near_up if way == 0 else near_down) + nx * feed
        z0 = (z - dist + nz) % nz if way == 0 else (z + dist) % nz
        x0, opposite = name(way, n // parts)
        comes = (dist < far) | ((dist == far) & opposite)
        goes = (dist < far - 1) | ((dist == far - 1) & opposite)
        return z0 // nx, x0, n % parts, comes, goes

    def relay(way, feed, n):
        y1, x0, j, comes, goes = chunk(way, feed, n)

        @pl.when(comes)
        def _():
            z_copy(way, y1, x0, j).wait_recv()

            @pl.when(goes)
            def _():
                z_copy(way, y1, x0, j).start()

            @pl.when(j == parts - 1)
            def _():
                deliver(y1, x0)

    @pl.loop(0, chunks + HOP * (far - 1))
    def _(step):
        for feed in range(feeds):
            for way, near in ((0, near_up), (1, near_down)):
                n = step - HOP * (near + nx * feed - 1)

                @pl.when((n >= 0) & (n < chunks))
                def _():
                    relay(way, feed, n)

    for u in range(ny):
        for v in range(1, nx):
            arrived(((y + u) % ny) * nx + (x + v) % nx)
    mine.wait()
    for fetch in fetches:
        fetch.wait()
    count, node, _ = a_ref.shape
    panel_rows, _, width = row_ref.shape
    agg = width // KP
    to = lax.broadcasted_iota(jnp.int32, (width, width), 0)
    at = lax.broadcasted_iota(jnp.int32, (width, width), 1)
    inner = to % agg
    source = to - inner + 2 * (inner % (agg // 2)) + inner // (agg // 2)
    pick = jnp.where(at == source, 1.0, 0.0).astype(BF16)

    @pl.loop(0, panel_rows // 8)
    def _(g):
        for i in range(8):
            turned[g * 8 + i] = lax.dot_general(
                pick, row_ref[g * 8 + i], (((1,), (1,)), ((), ())), preferred_element_type=F32
            ).astype(BF16)

    @pl.loop(0, count // GROUP)
    def _(g):
        for i in range(GROUP):
            k = g * GROUP + i
            left_ref[k] = jnp.dot(turned[rows_ref[k]], a_ref[k], preferred_element_type=F32).astype(BF16)

    def s_copy(c0):
        rows = col_ref.at[pl.ds(base + 2 * c0, 2)]
        return remote(rows, rows, s_send.at[c0], s_recv.at[c0], (sibling, c))

    @pl.loop(0, ncol)
    def _(i):
        c0 = (c + i) % ncol
        rows = col_ref.at[pl.ds(base + 2 * c0, 2)]
        remote(passing.at[0, 0], rows, a_send.at[0, 0], a_recv.at[c0], (r, c)).wait_recv()
        s_copy(c0).start()

    for copy in sends:
        copy.wait_send()

    @pl.when(jnp.logical_not(root))
    def _():
        gather_copy(x).wait_send()

    @pl.loop(0, nx)
    def _(x0):
        @pl.when(root)
        def _():
            for j in range(2 * PARTS):
                z_copy(0, plane, x0, j).wait_send()
                z_copy(1, plane, x0, j).wait_send()

        for y1 in range(ny):
            @pl.when(y1 != y)
            def _():
                a_copy(y1, x0).wait_send()

    @pl.loop(0, chunks)
    def _(n):
        for feed in range(feeds):
            for way in (0, 1):
                y1, x0, j, comes, goes = chunk(way, feed, n)

                @pl.when(comes & goes)
                def _():
                    z_copy(way, y1, x0, j).wait_send()

    @pl.loop(0, ncol)
    def _(c0):
        s_copy(c0).wait_send()
        s_copy(c0).wait_recv()


def panels(a_blocks, a_rows, p_blocks, dims):
    nz, ny, nx = dims
    ncol = ny * nx
    count = a_blocks.shape[0]
    _, node, width = p_blocks.shape
    vmem = pl.BlockSpec(memory_space=pltpu.VMEM)
    dma = pltpu.SemaphoreType.DMA
    return pl.pallas_call(
        functools.partial(panels_kernel, dims),
        out_shape=(
            jax.ShapeDtypeStruct((count, width, node), BF16),
            jax.ShapeDtypeStruct((4 * ncol, node, width), BF16),
        ),
        in_specs=[pl.BlockSpec(memory_space=pltpu.HBM)] * 3,
        out_specs=(vmem, vmem),
        scratch_shapes=[
            pltpu.SMEM(a_rows.shape, jnp.int32),
            pltpu.VMEM(a_blocks.shape, BF16),
            pltpu.VMEM((2 * ncol, node, width), BF16),
            pltpu.VMEM((2 * ncol, width, node), BF16),
            pltpu.VMEM((ny, nx, 2, node, width), BF16),
            dma((4,)),
            dma,
            dma((nx,)),
            dma((ncol - 1,)),
            dma((ncol,)),
            dma((2, ny, nx, 2 * PARTS)),
            dma((2, ny, nx, 2 * PARTS)),
            dma((ny, nx)),
            dma((ncol,)),
            dma((ncol,)),
            dma((ncol,)),
        ],
        compiler_params=pltpu.CompilerParams(collective_id=0, has_side_effects=True, vmem_limit_bytes=24 << 20),
        name="panels",
    )(*(pltpu.with_memory_space_constraint(v, pltpu.HBM) for v in (a_rows, a_blocks, p_blocks)))


def terms_kernel(cols_hbm, slots_hbm, left_ref, col_ref, out_ref, sem, cols_ref, slots_ref, *totals):
    count, width, _ = left_ref.shape
    agg = width // KP
    half = agg // 2
    fetches = [
        pltpu.make_async_copy(cols_hbm, cols_ref, sem.at[0]),
        pltpu.make_async_copy(slots_hbm, slots_ref, sem.at[1]),
    ]
    for fetch in fetches:
        fetch.start()

    @pl.loop(0, out_ref.shape[0] // 8)
    def _(g):
        some = pl.ds(pl.multiple_of(g * 8, 8), 8)
        for total in totals:
            total[some] = jnp.zeros((8, *total.shape[1:]), F32)

    for fetch in fetches:
        fetch.wait()

    low = lax.broadcasted_iota(jnp.int32, (half, 2 * agg), 1) < agg

    def block(k):
        term = jnp.dot(left_ref[k], col_ref[cols_ref[k]], preferred_element_type=F32)
        for pair in range(KP // 2):
            lanes = slice(pair * 2 * agg, (pair + 1) * 2 * agg)
            for t in range(KP):
                even = term[t * agg : t * agg + half, lanes]
                odd = term[t * agg + half : (t + 1) * agg, lanes]
                total = totals[t % len(totals)]
                total[slots_ref[t, 2 * pair, k]] += jnp.where(low, even, pltpu.roll(odd, agg, 1))
                total[slots_ref[t, 2 * pair + 1, k]] += jnp.where(low, pltpu.roll(even, agg, 1), odd)

    @pl.loop(0, count // GROUP)
    def _(g):
        for i in range(GROUP):
            block(g * GROUP + i)

    @pl.loop(0, out_ref.shape[0] // 8)
    def _(g):
        some = pl.ds(pl.multiple_of(g * 8, 8), 8)
        out_ref[some] = functools.reduce(lambda p, q: p + q, [total[some] for total in totals]).astype(BF16)


def local_terms(left, a_cols, slots, col_panel, slot_count):
    agg = left.shape[1] // KP
    slots = jnp.transpose(slots, (1, 2, 0))
    vmem, hbm = pl.BlockSpec(memory_space=pltpu.VMEM), pl.BlockSpec(memory_space=pltpu.HBM)
    return pl.pallas_call(
        functools.partial(terms_kernel),
        out_shape=jax.ShapeDtypeStruct((slot_count, agg // 2, 2 * agg), BF16),
        in_specs=[hbm, hbm, vmem, vmem],
        out_specs=vmem,
        scratch_shapes=[pltpu.SemaphoreType.DMA((2,))]
        + [pltpu.SMEM(ids.shape, jnp.int32) for ids in (a_cols, slots)]
        + [pltpu.VMEM((slot_count, agg // 2, 2 * agg), F32)] * 2,
        compiler_params=pltpu.CompilerParams(vmem_limit_bytes=24 << 20),
        name="terms",
    )(*(pltpu.with_memory_space_constraint(v, pltpu.HBM) for v in (a_cols, slots)), left, col_panel)


def sums_kernel(dims, part_ref, out_ref, landed, middle, last, send_sem, recv_sem, send_last, recv_last):
    _, ny, nx = dims
    r, c = lax.axis_index("row"), lax.axis_index("col")
    y, x = c // nx, c % nx
    half = out_ref.shape[0] // 2
    steps_x = [gray(v) for v in range(1, nx)]
    steps_y = [gray(v) for v in range(1, ny)]
    first, second = pl.ds(0, half), pl.ds(half, half)

    barrier = pltpu.get_barrier_semaphore()
    peers = [(r, y * nx + (x + d) % nx) for d in steps_x] + [(r, (y + d) % ny * nx + x) for d in steps_y]
    for peer in peers:
        pl.semaphore_signal(barrier, inc=1, device_id=peer, device_id_type=MESH)
    pl.semaphore_wait(barrier, len(peers))

    def remote(src, dst, send, recv, target):
        return pltpu.make_async_remote_copy(
            src_ref=src, dst_ref=dst, send_sem=send, recv_sem=recv, device_id=(r, target), device_id_type=MESH
        )

    def copy(way, d):
        if way == 0:
            x1 = (x + d) % nx
            src, target = part_ref.at[:, x1, first], y * nx + x1
        else:
            y1 = (y + d) % ny
            src, target = part_ref.at[y1, :, second], y1 * nx + x
        return remote(src, landed.at[way, d], send_sem.at[way, d], recv_sem.at[way, d], target)

    def copy_last(way, d):
        i = (y + d) % ny if way == 0 else (x + d) % nx
        target = i * nx + x if way == 0 else y * nx + i
        return remote(middle.at[way, d], last.at[way, d], send_last.at[way, d], recv_last.at[way, d], target)

    steps = (steps_x, steps_y)
    for dx, dy in zip(*steps):
        copy(0, dx).start()
        copy(1, dy).start()
    for way in (0, 1):
        for d in steps[way]:
            copy(way, d).wait_recv()

    def summed(way, i):
        own = part_ref[i, x, first] if way == 0 else part_ref[y, i, second]
        total = own.astype(F32)
        for d in steps[way]:
            total = total + landed[way, d, i].astype(F32)
        return total

    for dy, dx in zip(steps_y, steps_x):
        middle[0, dy] = summed(0, (y + dy) % ny)
        copy_last(0, dy).start()
        middle[1, dx] = summed(1, (x + dx) % nx)
        copy_last(1, dx).start()
    totals = [summed(0, y), summed(1, x)]
    for way in (0, 1):
        for d in steps[1 - way]:
            copy_last(way, d).wait_recv()
            totals[way] = totals[way] + last[way, d]
    total = jnp.concatenate(totals, axis=0)
    rows, lanes = total.shape[1:]
    for i in range(rows):
        out_ref[:, i * lanes : (i + 1) * lanes] = total[:, i, :].astype(BF16)
    for way in (0, 1):
        for d in steps[way]:
            copy(way, d).wait_send()
        for d in steps[1 - way]:
            copy_last(way, d).wait_send()


def sum_at_owner(partial, dims):
    _, ny, nx = dims
    assert ny == nx
    slots, rows, lanes = partial.shape
    share = slots // (ny * nx)
    half = (share // 2, rows, lanes)
    vmem = pl.BlockSpec(memory_space=pltpu.VMEM)
    dma = pltpu.SemaphoreType.DMA
    return pl.pallas_call(
        functools.partial(sums_kernel, dims),
        out_shape=jax.ShapeDtypeStruct((share, rows * lanes), BF16),
        in_specs=[vmem],
        out_specs=vmem,
        scratch_shapes=[
            pltpu.VMEM((2, nx, nx, *half), BF16),
            pltpu.VMEM((2, nx, *half), F32),
            pltpu.VMEM((2, nx, *half), F32),
            dma((2, nx)),
            dma((2, nx)),
            dma((2, nx)),
            dma((2, nx)),
        ],
        compiler_params=pltpu.CompilerParams(collective_id=1, has_side_effects=True, vmem_limit_bytes=16 << 20),
        name="sums",
    )(partial.reshape(ny, nx, share, rows, lanes))


def on_device(dims, slot_count, a_blocks, a_rows, a_cols, p_blocks, coarse_slot):
    left, col_panel = panels(a_blocks[0, 0], a_rows[0, 0], p_blocks, dims)
    partial = local_terms(left, a_cols[0, 0], coarse_slot[0, 0], col_panel, slot_count)
    return sum_at_owner(partial, dims)[None]


def solution(mesh, dims=(16, 4, 4), slot_count=128):
    placed = (
        P("row", "col", None, None, None),
        P("row", "col", None),
        P("row", "col", None),
        P(("row", "col"), None, None),
        P("row", "col", None, None, None),
    )
    return jax.shard_map(
        functools.partial(on_device, dims, slot_count),
        mesh=mesh,
        in_specs=placed,
        out_specs=P("row", "col", None),
        check_vma=False,
    )
```

```python
import functools

import jax
import jax.numpy as jnp
from jax import lax
from jax.experimental import pallas as pl
from jax.experimental.pallas import tpu as pltpu
from jax.sharding import PartitionSpec as P

MESH = pl.DeviceIdType.MESH
BF16, F32 = jnp.bfloat16, jnp.float32

HOP = 4
KP = 4
GROUP = 24
PARTS = 2


def gray(v):
    return v + v // 2 - 2 * ((v // 2) * (v % 2))


def panels_kernel(
    dims, rows_hbm, a_hbm, p_ref, left_ref, col_ref, rows_ref, a_ref, row_ref, turned, passing, own_sem, g_send, g_recv, r_send, r_recv, z_send, z_recv, a_send, a_recv, s_send, s_recv):
    nz, ny, nx = dims
    ncol = ny * nx
    r, c = lax.axis_index("row"), lax.axis_index("col")
    z, core = r // 2, r % 2
    y, x = c // nx, c % nx
    up, down = 2 * ((z + 1) % nz) + core, 2 * ((z + nz - 1) % nz) + core
    sibling = 2 * z + 1 - core
    base = core * 2 * ncol
    far = nz // 2
    steps_x = [gray(v) for v in range(1, nx)]
    steps_y = [gray(v) for v in range(1, ny)]

    def along_x(d):
        return y * nx + (x + d) % nx

    def along_y(d):
        return ((y + d) % ny) * nx + x

    barrier = pltpu.get_barrier_semaphore()
    peers = [(r, along_x(d)) for d in steps_x] + [(r, along_y(d)) for d in steps_y]
    peers += [(up, c), (down, c), (sibling, c)]
    for peer in peers:
        pl.semaphore_signal(barrier, inc=1, device_id=peer, device_id_type=MESH)
    pl.semaphore_wait(barrier, len(peers))

    def remote(src, dst, send, recv, device):
        return pltpu.make_async_remote_copy(
            src_ref=src, dst_ref=dst, send_sem=send, recv_sem=recv, device_id=device, device_id_type=MESH
        )

    root = x == z % nx
    plane = z // nx

    def gather_copy(x0):
        return remote(p_ref, passing.at[plane, x0], g_send, g_recv.at[x0], (r, y * nx + z % nx))

    part = p_ref.shape[1] // PARTS

    def z_copy(way, y1, x0, j):
        here = passing.at[y1, x0, j // PARTS, pl.ds(pl.multiple_of(j % PARTS * part, part), part)]
        return remote(here, here, z_send.at[way, y1, x0, j], z_recv.at[way, y1, x0, j], (up if way == 0 else down, c))

    def name(way, pos):
        o = pos if way == 0 else (nx - pos) % nx
        return (x + o) % nx, (o < nx // 2 if way == 0 else o >= nx // 2)

    def a_copy(y1, x0, row):
        piece = y * nx + x0
        dst = col_ref.at[base + 2 * piece + row]
        return remote(passing.at[y1, x0, row], dst, a_send.at[y1, x0, row], a_recv.at[piece, row], (r, y1 * nx + x))

    def deliver(y1, x0, row):
        @pl.when(y1 != y)
        def _():
            a_copy(y1, x0, row).start()

        @pl.when(y1 == y)
        def _():
            piece = y * nx + x0
            dst = col_ref.at[base + 2 * piece + row]
            pltpu.make_async_copy(passing.at[y1, x0, row], dst, a_recv.at[piece, row]).start()

    sends = []

    def give(src, piece, target):
        rows = row_ref.at[pl.ds(2 * piece, 2)]
        copy = remote(src, rows, r_send.at[len(sends)], r_recv.at[piece], (r, target))
        copy.start()
        sends.append(copy)

    def arrived(piece):
        rows = row_ref.at[pl.ds(2 * piece, 2)]
        remote(rows, rows, r_send.at[0], r_recv.at[piece], (r, c)).wait_recv()

    @pl.when(jnp.logical_not(root))
    def _():
        gather_copy(x).start()

    @pl.when(root)
    def _():
        copy = pltpu.make_async_copy(p_ref, passing.at[plane, x], own_sem.at[1])
        copy.start()
        copy.wait()
        for j in range(2 * PARTS):
            z_copy(0, plane, x, j).start()
            z_copy(1, plane, x, j).start()
        deliver(plane, x, 0)
        deliver(plane, x, 1)

    fetches = [
        pltpu.make_async_copy(rows_hbm, rows_ref, own_sem.at[2]),
        pltpu.make_async_copy(a_hbm, a_ref, own_sem.at[3]),
    ]
    for fetch in fetches:
        fetch.start()
    mine = pltpu.make_async_copy(p_ref, row_ref.at[pl.ds(2 * c, 2)], own_sem.at[0])
    mine.start()
    for d in steps_y:
        give(p_ref, c, along_y(d))
    for d in steps_x:
        give(p_ref, c, along_x(d))

    @pl.when(root)
    def _():
        for pos in range(1, nx):
            a, b = name(0, pos)[0], name(1, pos)[0]
            if 2 * pos <= nx:
                gather_copy(a).wait_recv()
                if 2 * pos < nx:
                    gather_copy(b).wait_recv()
            for j in range(2 * PARTS):
                z_copy(0, plane, a, j).start()
                z_copy(1, plane, b, j).start()
            deliver(plane, a, 0)
            deliver(plane, a, 1)

    for d in steps_y:
        piece = along_y(d)
        arrived(piece)
        for e in steps_x:
            give(row_ref.at[pl.ds(2 * piece, 2)], piece, along_x(e))

    near_up = (z - x + nz - 1) % nx + 1
    near_down = (x - z + nz - 1) % nx + 1
    feeds, parts = far // nx, 2 * PARTS
    chunks = nx * parts

    def chunk(way, feed, n):
        dist = (near_up if way == 0 else near_down) + nx * feed
        z0 = (z - dist + nz) % nz if way == 0 else (z + dist) % nz
        x0, opposite = name(way, n // parts)
        comes = (dist < far) | ((dist == far) & opposite)
        goes = (dist < far - 1) | ((dist == far - 1) & opposite)
        return z0 // nx, x0, n % parts, comes, goes

    def relay(way, feed, n):
        y1, x0, j, comes, goes = chunk(way, feed, n)

        @pl.when(comes)
        def _():
            z_copy(way, y1, x0, j).wait_recv()

            @pl.when(goes)
            def _():
                z_copy(way, y1, x0, j).start()

            @pl.when(j % PARTS == PARTS - 1)
            def _():
                deliver(y1, x0, j // PARTS)

    @pl.loop(0, chunks + HOP * (far - 1))
    def _(step):
        for feed in range(feeds):
            for way, near in ((0, near_up), (1, near_down)):
                n = step - HOP * (near + nx * feed - 1)

                @pl.when((n >= 0) & (n < chunks))
                def _():
                    relay(way, feed, n)

    for u in range(ny):
        for v in range(1, nx):
            arrived(((y + u) % ny) * nx + (x + v) % nx)
    mine.wait()
    for fetch in fetches:
        fetch.wait()
    count, node, _ = a_ref.shape
    panel_rows, _, width = row_ref.shape
    agg = width // KP
    to = lax.broadcasted_iota(jnp.int32, (width, width), 0)
    at = lax.broadcasted_iota(jnp.int32, (width, width), 1)
    inner = to % agg
    source = to - inner + 2 * (inner % (agg // 2)) + inner // (agg // 2)
    pick = jnp.where(at == source, 1.0, 0.0).astype(BF16)

    @pl.loop(0, panel_rows // 8)
    def _(g):
        for i in range(8):
            turned[g * 8 + i] = lax.dot_general(
                pick, row_ref[g * 8 + i], (((1,), (1,)), ((), ())), preferred_element_type=F32
            ).astype(BF16)

    @pl.loop(0, count // GROUP)
    def _(g):
        for i in range(GROUP):
            k = g * GROUP + i
            left_ref[k] = jnp.dot(turned[rows_ref[k]], a_ref[k], preferred_element_type=F32).astype(BF16)

    def s_copy(c0):
        rows = col_ref.at[pl.ds(base + 2 * c0, 2)]
        return remote(rows, rows, s_send.at[c0], s_recv.at[c0], (sibling, c))

    @pl.loop(0, ncol)
    def _(i):
        c0 = (c + i) % ncol
        for row in (0, 1):
            here = col_ref.at[base + 2 * c0 + row]
            remote(here, here, a_send.at[0, 0, 0], a_recv.at[c0, row], (r, c)).wait_recv()
        s_copy(c0).start()

    for copy in sends:
        copy.wait_send()

    @pl.when(jnp.logical_not(root))
    def _():
        gather_copy(x).wait_send()

    @pl.loop(0, nx)
    def _(x0):
        @pl.when(root)
        def _():
            for j in range(2 * PARTS):
                z_copy(0, plane, x0, j).wait_send()
                z_copy(1, plane, x0, j).wait_send()

        for y1 in range(ny):
            @pl.when(y1 != y)
            def _():
                a_copy(y1, x0, 0).wait_send()
                a_copy(y1, x0, 1).wait_send()

    @pl.loop(0, chunks)
    def _(n):
        for feed in range(feeds):
            for way in (0, 1):
                y1, x0, j, comes, goes = chunk(way, feed, n)

                @pl.when(comes & goes)
                def _():
                    z_copy(way, y1, x0, j).wait_send()

    @pl.loop(0, ncol)
    def _(c0):
        s_copy(c0).wait_send()
        s_copy(c0).wait_recv()


def panels(a_blocks, a_rows, p_blocks, dims):
    nz, ny, nx = dims
    ncol = ny * nx
    count = a_blocks.shape[0]
    _, node, width = p_blocks.shape
    vmem = pl.BlockSpec(memory_space=pltpu.VMEM)
    dma = pltpu.SemaphoreType.DMA
    return pl.pallas_call(
        functools.partial(panels_kernel, dims),
        out_shape=(
            jax.ShapeDtypeStruct((count, width, node), BF16),
            jax.ShapeDtypeStruct((4 * ncol, node, width), BF16),
        ),
        in_specs=[pl.BlockSpec(memory_space=pltpu.HBM)] * 3,
        out_specs=(vmem, vmem),
        scratch_shapes=[
            pltpu.SMEM(a_rows.shape, jnp.int32),
            pltpu.VMEM(a_blocks.shape, BF16),
            pltpu.VMEM((2 * ncol, node, width), BF16),
            pltpu.VMEM((2 * ncol, width, node), BF16),
            pltpu.VMEM((ny, nx, 2, node, width), BF16),
            dma((4,)),
            dma,
            dma((nx,)),
            dma((ncol - 1,)),
            dma((ncol,)),
            dma((2, ny, nx, 2 * PARTS)),
            dma((2, ny, nx, 2 * PARTS)),
            dma((ny, nx, 2)),
            dma((ncol, 2)),
            dma((ncol,)),
            dma((ncol,)),
        ],
        compiler_params=pltpu.CompilerParams(collective_id=0, has_side_effects=True, vmem_limit_bytes=24 << 20),
        name="panels",
    )(*(pltpu.with_memory_space_constraint(v, pltpu.HBM) for v in (a_rows, a_blocks, p_blocks)))


def terms_kernel(cols_hbm, slots_hbm, left_ref, col_ref, out_ref, sem, cols_ref, slots_ref, *totals):
    count, width, _ = left_ref.shape
    agg = width // KP
    half = agg // 2
    fetches = [
        pltpu.make_async_copy(cols_hbm, cols_ref, sem.at[0]),
        pltpu.make_async_copy(slots_hbm, slots_ref, sem.at[1]),
    ]
    for fetch in fetches:
        fetch.start()

    @pl.loop(0, out_ref.shape[0] // 8)
    def _(g):
        some = pl.ds(pl.multiple_of(g * 8, 8), 8)
        for total in totals:
            total[some] = jnp.zeros((8, *total.shape[1:]), F32)

    for fetch in fetches:
        fetch.wait()

    low = lax.broadcasted_iota(jnp.int32, (half, 2 * agg), 1) < agg

    def block(k):
        term = jnp.dot(left_ref[k], col_ref[cols_ref[k]], preferred_element_type=F32)
        for pair in range(KP // 2):
            lanes = slice(pair * 2 * agg, (pair + 1) * 2 * agg)
            for t in range(KP):
                even = term[t * agg : t * agg + half, lanes]
                odd = term[t * agg + half : (t + 1) * agg, lanes]
                total = totals[t % len(totals)]
                total[slots_ref[t, 2 * pair, k]] += jnp.where(low, even, pltpu.roll(odd, agg, 1))
                total[slots_ref[t, 2 * pair + 1, k]] += jnp.where(low, pltpu.roll(even, agg, 1), odd)

    @pl.loop(0, count // GROUP)
    def _(g):
        for i in range(GROUP):
            block(g * GROUP + i)

    @pl.loop(0, out_ref.shape[0] // 8)
    def _(g):
        some = pl.ds(pl.multiple_of(g * 8, 8), 8)
        out_ref[some] = functools.reduce(lambda p, q: p + q, [total[some] for total in totals]).astype(BF16)


def local_terms(left, a_cols, slots, col_panel, slot_count):
    agg = left.shape[1] // KP
    slots = jnp.transpose(slots, (1, 2, 0))
    vmem, hbm = pl.BlockSpec(memory_space=pltpu.VMEM), pl.BlockSpec(memory_space=pltpu.HBM)
    return pl.pallas_call(
        functools.partial(terms_kernel),
        out_shape=jax.ShapeDtypeStruct((slot_count, agg // 2, 2 * agg), BF16),
        in_specs=[hbm, hbm, vmem, vmem],
        out_specs=vmem,
        scratch_shapes=[pltpu.SemaphoreType.DMA((2,))]
        + [pltpu.SMEM(ids.shape, jnp.int32) for ids in (a_cols, slots)]
        + [pltpu.VMEM((slot_count, agg // 2, 2 * agg), F32)] * 2,
        compiler_params=pltpu.CompilerParams(vmem_limit_bytes=24 << 20),
        name="terms",
    )(*(pltpu.with_memory_space_constraint(v, pltpu.HBM) for v in (a_cols, slots)), left, col_panel)


def sums_kernel(dims, part_ref, out_ref, landed, middle, last, send_sem, recv_sem, send_last, recv_last):
    _, ny, nx = dims
    r, c = lax.axis_index("row"), lax.axis_index("col")
    y, x = c // nx, c % nx
    half = out_ref.shape[0] // 2
    steps_x = [gray(v) for v in range(1, nx)]
    steps_y = [gray(v) for v in range(1, ny)]
    first, second = pl.ds(0, half), pl.ds(half, half)

    barrier = pltpu.get_barrier_semaphore()
    peers = [(r, y * nx + (x + d) % nx) for d in steps_x] + [(r, (y + d) % ny * nx + x) for d in steps_y]
    for peer in peers:
        pl.semaphore_signal(barrier, inc=1, device_id=peer, device_id_type=MESH)
    pl.semaphore_wait(barrier, len(peers))

    def remote(src, dst, send, recv, target):
        return pltpu.make_async_remote_copy(
            src_ref=src, dst_ref=dst, send_sem=send, recv_sem=recv, device_id=(r, target), device_id_type=MESH
        )

    def copy(way, d, e):
        if way == 0:
            i, x1 = (y + e) % ny, (x + d) % nx
            src, target = part_ref.at[i, x1, first], y * nx + x1
        else:
            i, y1 = (x + e) % nx, (y + d) % ny
            src, target = part_ref.at[y1, i, second], y1 * nx + x
        return remote(src, landed.at[way, d, i], send_sem.at[way, d, e], recv_sem.at[way, d, e], target)

    def copy_last(way, d):
        i = (y + d) % ny if way == 0 else (x + d) % nx
        target = i * nx + x if way == 0 else y * nx + i
        return remote(middle.at[way, d], last.at[way, d], send_last.at[way, d], recv_last.at[way, d], target)

    steps = (steps_x, steps_y)
    for e in (*steps_y, 0):
        for dx, dy in zip(*steps):
            copy(0, dx, e).start()
            copy(1, dy, e).start()

    def summed(way, e):
        for d in steps[way]:
            copy(way, d, e).wait_recv()
        i = (y + e) % ny if way == 0 else (x + e) % nx
        own = part_ref[i, x, first] if way == 0 else part_ref[y, i, second]
        total = own.astype(F32)
        for d in steps[way]:
            total = total + landed[way, d, i].astype(F32)
        return total

    for dy, dx in zip(steps_y, steps_x):
        middle[0, dy] = summed(0, dy)
        copy_last(0, dy).start()
        middle[1, dx] = summed(1, dx)
        copy_last(1, dx).start()
    totals = [summed(0, 0), summed(1, 0)]
    for way in (0, 1):
        for d in steps[1 - way]:
            copy_last(way, d).wait_recv()
            totals[way] = totals[way] + last[way, d]
    total = jnp.concatenate(totals, axis=0)
    rows, lanes = total.shape[1:]
    for i in range(rows):
        out_ref[:, i * lanes : (i + 1) * lanes] = total[:, i, :].astype(BF16)
    for way in (0, 1):
        for d in steps[way]:
            for e in range(nx):
                copy(way, d, e).wait_send()
        for d in steps[1 - way]:
            copy_last(way, d).wait_send()


def sum_at_owner(partial, dims):
    _, ny, nx = dims
    assert ny == nx
    slots, rows, lanes = partial.shape
    share = slots // (ny * nx)
    half = (share // 2, rows, lanes)
    vmem = pl.BlockSpec(memory_space=pltpu.VMEM)
    dma = pltpu.SemaphoreType.DMA
    return pl.pallas_call(
        functools.partial(sums_kernel, dims),
        out_shape=jax.ShapeDtypeStruct((share, rows * lanes), BF16),
        in_specs=[vmem],
        out_specs=vmem,
        scratch_shapes=[
            pltpu.VMEM((2, nx, nx, *half), BF16),
            pltpu.VMEM((2, nx, *half), F32),
            pltpu.VMEM((2, nx, *half), F32),
            dma((2, nx, nx)),
            dma((2, nx, nx)),
            dma((2, nx)),
            dma((2, nx)),
        ],
        compiler_params=pltpu.CompilerParams(collective_id=1, has_side_effects=True, vmem_limit_bytes=16 << 20),
        name="sums",
    )(partial.reshape(ny, nx, share, rows, lanes))


def on_device(dims, slot_count, a_blocks, a_rows, a_cols, p_blocks, coarse_slot):
    left, col_panel = panels(a_blocks[0, 0], a_rows[0, 0], p_blocks, dims)
    partial = local_terms(left, a_cols[0, 0], coarse_slot[0, 0], col_panel, slot_count)
    return sum_at_owner(partial, dims)[None]


def solution(mesh, dims=(16, 4, 4), slot_count=128):
    placed = (
        P("row", "col", None, None, None),
        P("row", "col", None),
        P("row", "col", None),
        P(("row", "col"), None, None),
        P("row", "col", None, None, None),
    )
    return jax.shard_map(
        functools.partial(on_device, dims, slot_count),
        mesh=mesh,
        in_specs=placed,
        out_specs=P("row", "col", None),
        check_vma=False,
    )
```
